32 devices in a mesh: seq: 8 (over z, y), head: 4 (over x, core).
Axes of the slice: x: 2, y: 2, z: 4, core: 2. Of those that a mesh axis runs over, the one named last changes fastest.
Arguments:
- tokens: bfloat16 [4096, 2048], P('seq'), may hold values from -6 to 6
- w_query: bfloat16 [2048, 2048], P('seq', 'head'), may hold values from -0.125 to 0.125
- w_key: bfloat16 [2048, 2048], P('seq', 'head'), may hold values from -0.125 to 0.125
- w_value: bfloat16 [2048, 2048], P('seq', 'head'), may hold values from -0.125 to 0.125
- w_out: bfloat16 [2048, 2048], P('head', 'seq'), may hold values from -0.125 to 0.125
- level_weights: float32 [16, 13, 4096], P('head', None, 'seq'), may hold values from 0.2 to 2
Outputs:
- layer_output: bfloat16 [4096, 2048], P('seq', 'head')
The draws below stay inside these ranges and needn't reach their ends.
All inputs are finite; a program needn't handle non-finite values.
Results may differ from the reference program's by a relative error of at most 0.017.
Values may be sent and summed in bfloat16 or wider, within the bound.
No kernel may reach another device: no remote copies, remote signals or barrier semaphores. Data moves between devices by JAX's collectives and lax.ppermute only.
A program may use at most 128 MiB of HBM per device.

```python
import math
import jax
import jax.numpy as jnp
from jax import lax

D = 2048
HEADS = 16
HEAD_DIM = 128
TOK_DEV = 512
TOKENS = 4096
LEVELS = 13
N_SEQ = 8
N_HEAD = 4


def steps_of(key, extent, split, smallest, high):
    def one(position, blocks):
        draws = jax.random.uniform(jax.random.fold_in(jax.random.fold_in(key, 6), position), (blocks,), jnp.float32, smallest / len(split), high / len(split))
        return jnp.repeat(jnp.exp(draws), extent[position] // blocks).reshape((-1,) + (1,) * (len(extent) - position - 1))

    level = one(*split[0])
    for cut in split[1:]:
        level = level * one(*cut)
    return level


def centred(key, dims, spread, bound, split=(), kind=jnp.bfloat16):
    drawn = jax.random.normal(key, dims, jnp.float32) * spread
    if len(split) > 0:
        drawn = steps_of(key, dims, split, -0.22, 0.18) * drawn
    return jnp.clip(drawn, min=-bound, max=bound).astype(kind)


def setup_inputs(seed: int = 0) -> dict:
    key_list = jax.random.split(jax.random.key(seed), 7)
    tokens = centred(key_list[0], (TOKENS, D), 1.0, 6.0, ((0, 8),))
    w_query = centred(key_list[1], (D, HEADS * HEAD_DIM), D ** -0.5, 0.125, ((0, 8), (1, 4)))
    w_key = centred(key_list[2], (D, HEADS * HEAD_DIM), D ** -0.5, 0.125, ((0, 8), (1, 4)))
    w_value = centred(key_list[3], (D, HEADS * HEAD_DIM), D ** -0.5, 0.125, ((0, 8), (1, 4)))
    w_out = centred(key_list[4], (HEADS * HEAD_DIM, D), (HEADS * HEAD_DIM) ** -0.5, 0.125, ((0, 4), (1, 8)))
    level_weights = jnp.clip(jnp.exp(math.log(2.0) - 2.3025851 * jax.random.uniform(key_list[5], (HEADS, LEVELS, TOKENS), jnp.float32) ** steps_of(key_list[5], (HEADS, LEVELS, TOKENS), ((0, 4), (2, 8)), -0.2, 0.2)), 0.2, 2.0)
    return dict(tokens=tokens, w_query=w_query, w_key=w_key, w_value=w_value, w_out=w_out, level_weights=level_weights)


def bit_length(numbers, bit_count):
    total_bits = jnp.zeros(numbers.shape, jnp.int32)
    for bit_index in range(bit_count):
        total_bits = total_bits + (numbers >= 1 << bit_index).astype(jnp.int32)
    return total_bits

def reference(tokens, w_query, w_key, w_value, w_out, level_weights):
    highest = lax.Precision.HIGHEST
    local_bits = TOK_DEV.bit_length() - 1
    block_shape = (N_SEQ, TOK_DEV, HEADS, HEAD_DIM)
    query_vectors = jnp.dot(tokens, w_query, preferred_element_type=jnp.float32).astype(jnp.bfloat16).reshape(block_shape)
    key_vectors = jnp.dot(tokens, w_key, preferred_element_type=jnp.float32).astype(jnp.bfloat16).reshape(block_shape)
    value_vectors = jnp.dot(tokens, w_value, preferred_element_type=jnp.float32).astype(jnp.bfloat16).reshape(block_shape)
    weights_blocked = level_weights.reshape(HEADS, LEVELS, N_SEQ, TOK_DEV).transpose(2, 0, 1, 3)
    states = jnp.einsum('bchd,bche->bhde', key_vectors.astype(jnp.float32), value_vectors.astype(jnp.float32), precision=highest)
    query_float = query_vectors.astype(jnp.float32)
    remote_part = jnp.zeros(block_shape, jnp.float32)
    running = states
    device_order = jnp.arange(N_SEQ, dtype=jnp.int32)
    for bit_index in range(N_SEQ.bit_length() - 1):
        partner = jnp.take(running, jnp.bitwise_xor(device_order, jnp.int32(1 << bit_index)), axis=0)
        upper_half = jnp.bitwise_and(jnp.right_shift(device_order, bit_index), 1).astype(jnp.float32)
        scaled = weights_blocked[:, :, local_bits + bit_index + 1, :].transpose(0, 2, 1)[..., None] * query_float
        term = jnp.einsum('bchd,bhde->bche', scaled, partner, precision=highest)
        remote_part = remote_part + upper_half[:, None, None, None] * term
        running = running + partner
    positions = jnp.arange(TOK_DEV, dtype=jnp.int32)
    levels = bit_length(jnp.bitwise_xor(positions[:, None], positions[None, :]), local_bits)
    causal = positions[None, :] <= positions[:, None]

    def inside(block_items):
        query_block, key_block, value_block, weight_block = block_items
        scores = jnp.einsum('thd,shd->hts', query_block.astype(jnp.float32), key_block.astype(jnp.float32), precision=highest)
        mixing = jnp.zeros_like(scores)
        for level_index in range(local_bits + 1):
            mixing = mixing + weight_block[:, level_index, :, None] * (levels == level_index).astype(jnp.float32)
        mixing = jnp.where(causal, mixing, jnp.zeros_like(mixing))
        weighted = (scores * mixing).astype(jnp.bfloat16)
        return jnp.einsum('hts,shd->thd', weighted.astype(jnp.float32), value_block.astype(jnp.float32), precision=highest)
    local_part = lax.map(inside, (query_vectors, key_vectors, value_vectors, weights_blocked))
    combined = local_part + remote_part
    attended = combined * lax.rsqrt(lax.optimization_barrier(jnp.mean(combined * combined, axis=-1, keepdims=True)) + 1e-06)
    attended = attended.astype(jnp.bfloat16).reshape(TOKENS, HEADS * HEAD_DIM)
    group_width = HEADS * HEAD_DIM // N_HEAD
    summed = jnp.zeros((TOKENS, D), jnp.float32)
    for group_index in range(N_HEAD):
        lower = group_index * group_width
        partial_value = jnp.dot(attended[:, lower:lower + group_width], w_out[lower:lower + group_width], preferred_element_type=jnp.float32)
        summed = summed + lax.optimization_barrier(partial_value.astype(jnp.bfloat16)).astype(jnp.float32)
    return summed.astype(jnp.bfloat16)
```

```python
import functools

import jax
import jax.numpy as jnp
from jax import lax
from jax.experimental import pallas as pl
from jax.experimental.pallas import tpu as pltpu
from jax.sharding import PartitionSpec as P

F32, BF16 = jnp.float32, jnp.bfloat16
LONGEST_RING = 16
VMEM = pl.BlockSpec(memory_space=pltpu.VMEM)
SMEM = pl.BlockSpec(memory_space=pltpu.SMEM)


def call(kernel, outs, operands, flops, scratch=(), **grid):
    nbytes = sum(a.size * a.dtype.itemsize for a in (*operands, *outs))
    return pl.pallas_call(
        kernel,
        out_shape=outs,
        scratch_shapes=list(scratch),
        compiler_params=pltpu.CompilerParams(vmem_limit_bytes=48 * 2**20),
        cost_estimate=pl.CostEstimate(flops=flops, bytes_accessed=nbytes, transcendentals=0),
        **grid,
    )(*operands)


def ring_order(n):
    return list(range(0, n, 2)) + list(range(n - 1, 0, -2))


def ring_position(index, n):
    return jnp.where(index % 2 == 0, index // 2, n - 1 - index // 2)


def ring_owner(position, n):
    position = (position + n) % n
    return jnp.where(position < n // 2, 2 * position, 2 * (n - 1 - position) + 1)


def gather_pieces(piece, n):
    order = ring_order(n)
    onward = [(order[i], order[(i + 1) % n]) for i in range(n)]
    back = [(b, a) for a, b in onward]
    here = ring_position(lax.axis_index("seq"), n)
    pieces = [(piece, lax.axis_index("seq"), 0)]
    up = down = piece
    for step in range(1, n // 2):
        up = lax.ppermute(up, "seq", onward)
        down = lax.ppermute(down, "seq", back)
        pieces.append((up, ring_owner(here - step, n), 0))
        pieces.append((down, ring_owner(here + step, n), 0))
    half = piece.shape[0] // 2
    last = ring_owner(here + n // 2, n)
    pieces.append((lax.ppermute(up[:half], "seq", onward), last, 0))
    pieces.append((lax.ppermute(down[half:], "seq", back), last, half))
    return pieces


def gather_rows(piece, n):
    if n > LONGEST_RING or n % 2:
        return [(lax.all_gather(piece, "seq", axis=0, tiled=True), jnp.int32(0))]
    rows = piece.shape[0]
    return [(a, owner * rows + first) for a, owner, first in gather_pieces(piece, n)]


def place(starts, pieces, whole):
    for i, piece in enumerate(pieces):
        rows = piece.shape[0]
        whole[pl.ds(pl.multiple_of(starts[i], rows), rows), :] = piece[...]


def project_kernel(starts, tokens, *refs):
    *pieces, out, whole = refs
    place(starts, pieces, whole)
    width = min(256, out.shape[1])
    for low in range(0, out.shape[1], width):
        cols = slice(low, low + width)
        out[:, cols] = jnp.dot(
            tokens[...], whole[:, cols], preferred_element_type=F32
        ).astype(BF16)


def project(tokens, pieces):
    arrays = [a for a, _ in pieces]
    starts = jnp.stack([jnp.asarray(s, jnp.int32) for _, s in pieces])
    rows, depth = tokens.shape
    width = arrays[0].shape[1]
    return call(
        project_kernel,
        [jax.ShapeDtypeStruct((rows, width), BF16)],
        [starts, tokens, *arrays],
        2 * rows * depth * width,
        [pltpu.VMEM((depth, width), BF16)],
        in_specs=[SMEM, VMEM] + [VMEM] * len(arrays),
        out_specs=[VMEM],
    )[0]


def states_kernel(keys, values, states, rounded):
    for h in range(states.shape[0]):
        cols = slice(h * states.shape[1], (h + 1) * states.shape[1])
        sums = lax.dot_general(
            keys[:, cols], values[:, cols], (((0,), (0,)), ((), ())), preferred_element_type=F32
        )
        states[h] = sums
        rounded[h] = sums.astype(BF16)


def key_value_states(keys, values, heads):
    rows, width = keys.shape
    shape = (heads, width // heads, width // heads)
    return call(
        states_kernel,
        [jax.ShapeDtypeStruct(shape, F32), jax.ShapeDtypeStruct(shape, BF16)],
        [keys, values],
        2 * rows * width * shape[-1],
        in_specs=[VMEM] * 2,
        out_specs=[VMEM] * 2,
    )


def mixing_kernel(bits, weights, mixing):
    rows = mixing.shape[1]
    tile = min(256, rows)
    tile_bits = tile.bit_length() - 1
    column = lambda level, low: weights[0, low : low + tile, level : level + 1]
    t = lax.broadcasted_iota(jnp.int32, (tile, tile), 0)
    s = lax.broadcasted_iota(jnp.int32, (tile, tile), 1)
    apart = jnp.bitwise_xor(t, s)
    for low in range(0, rows, tile):
        for left in range(0, low, tile):
            level = tile_bits + ((low // tile) ^ (left // tile)).bit_length()
            mixing[0, low : low + tile, left : left + tile] = jnp.broadcast_to(
                column(level, low), (tile, tile)
            )
        mixed = jnp.broadcast_to(column(0, low), (tile, tile))
        for level in range(1, tile_bits + 1):
            mixed = jnp.where(apart >= 1 << (level - 1), column(level, low), mixed)
        mixing[0, low : low + tile, low : low + tile] = jnp.where(s <= t, mixed, 0.0)


def mixing_matrix(weights_by_token, bits):
    heads, rows, levels = weights_by_token.shape
    return call(
        functools.partial(mixing_kernel, bits),
        [jax.ShapeDtypeStruct((heads, rows, rows), F32)],
        [weights_by_token],
        heads * rows * rows * 10,
        grid=(heads,),
        in_specs=[pl.BlockSpec((1, rows, levels), lambda h: (h, 0, 0))],
        out_specs=[pl.BlockSpec((1, rows, rows), lambda h: (h, 0, 0))],
    )[0]


def attend_kernel(first_level, queries, keys, values, mixing, weights, *refs):
    *states, out = refs
    rows = queries.shape[0]
    tile = min(256, rows)
    for low in range(0, rows, tile):
        high = low + tile
        query = queries[low:high, :]
        scores = lax.dot_general(
            query, keys[:high, :], (((1,), (1,)), ((), ())), preferred_element_type=F32
        )
        mixed = (scores * mixing[0, low:high, :high]).astype(BF16)
        total = jnp.dot(mixed, values[:high, :], preferred_element_type=F32)
        for bit, state in enumerate(states):
            level = first_level + bit
            total += weights[0, low:high, level : level + 1] * jnp.dot(
                query, state[0], preferred_element_type=F32
            )
        scale = lax.rsqrt(jnp.mean(total * total, axis=-1, keepdims=True) + 1e-06)
        out[low:high, :] = (total * scale).astype(BF16)


def attend(queries, keys, values, mixing, weights_by_token, states, first_level):
    rows, width = queries.shape
    heads, _, levels = weights_by_token.shape
    dim = width // heads
    by_head = pl.BlockSpec((rows, dim), lambda h: (0, h))
    return call(
        functools.partial(attend_kernel, first_level),
        [jax.ShapeDtypeStruct((rows, width), BF16)],
        [queries, keys, values, mixing, weights_by_token, *states],
        heads * (4 * rows * rows * dim + 6 * rows * dim * dim),
        grid=(heads,),
        in_specs=[by_head] * 3
        + [
            pl.BlockSpec((1, rows, rows), lambda h: (h, 0, 0)),
            pl.BlockSpec((1, rows, levels), lambda h: (h, 0, 0)),
        ]
        + [pl.BlockSpec((1, dim, dim), lambda h: (h, 0, 0))] * len(states),
        out_specs=[by_head],
    )[0]


def output_kernel(count, starts, *refs):
    attended, pieces, (out, whole) = refs[:count], refs[count:-2], refs[-2:]
    for i, piece in enumerate(pieces):
        rows, cols = piece.shape
        down = pl.ds(pl.multiple_of(starts[0, i], rows), rows)
        along = pl.ds(pl.multiple_of(starts[1, i], cols), cols)
        whole[down, along] = piece[...]
    depth = attended[0].shape[1]
    total = jnp.zeros(out.shape, F32)
    for i, block in enumerate(attended):
        total += jnp.dot(
            block[...], whole[i * depth : (i + 1) * depth, :], preferred_element_type=F32
        )
    out[...] = total.astype(BF16)


def output(attended, pieces):
    arrays = [a for a, _, _ in pieces]
    starts = jnp.stack(
        [jnp.stack([jnp.asarray(p[i], jnp.int32) for p in pieces]) for i in (1, 2)]
    )
    rows, part = attended[0].shape
    depth = part * len(attended)
    width = sum(a.size for a in arrays) // depth
    return call(
        functools.partial(output_kernel, len(attended)),
        [jax.ShapeDtypeStruct((rows, width), BF16)],
        [starts, *attended, *arrays],
        2 * rows * depth * width,
        [pltpu.VMEM((depth, width), BF16)],
        in_specs=[SMEM] + [VMEM] * (len(attended) + len(arrays)),
        out_specs=[VMEM],
    )[0]


def per_device(tokens, w_query, w_key, w_value, w_out, level_weights):
    n = lax.axis_size("seq")
    groups = lax.axis_size("head")
    here = lax.axis_index("seq")
    group = lax.axis_index("head")
    rows = tokens.shape[0]
    local_bits = rows.bit_length() - 1
    heads = level_weights.shape[0]

    share = n // groups
    moves = [
        (s * groups + h, (s % share * groups + h) * groups + s // share)
        for s in range(n)
        for h in range(groups)
    ]
    out_piece = lax.ppermute(w_out, ("seq", "head"), moves)

    weights_by_token = level_weights.transpose(0, 2, 1)
    mixing = mixing_matrix(weights_by_token, local_bits)

    keys = project(tokens, gather_rows(w_key, n))
    values = project(tokens, gather_rows(w_value, n))
    running, rounded = key_value_states(keys, values, heads)
    states = []
    for bit in range(n.bit_length() - 1):
        partner = lax.ppermute(rounded, "seq", [(i, i ^ 1 << bit) for i in range(n)])
        upper = jnp.bitwise_and(jnp.right_shift(here, bit), 1)
        states.append(partner * upper.astype(BF16))
        running = running + partner.astype(F32)
        rounded = running.astype(BF16)
    queries = project(tokens, gather_rows(w_query, n))
    attended = attend(
        queries, keys, values, mixing, weights_by_token, states, local_bits + 1
    )

    blocks = {0: attended}
    for bit in reversed(range(groups.bit_length() - 1)):
        pairs = [(i, i ^ 1 << bit) for i in range(groups)]
        blocks |= {k ^ 1 << bit: lax.ppermute(a, "head", pairs) for k, a in blocks.items()}
    blocks = [blocks[k] for k in range(groups)]

    depth = w_out.shape[0]
    if n > LONGEST_RING or n % 2:
        gathered = lax.all_gather(out_piece, "seq", axis=0)
        gathered = gathered.reshape(share, groups, depth, -1).transpose(1, 2, 0, 3)
        gathered = gathered.reshape(groups, depth, -1)
        pieces = [
            (lax.dynamic_index_in_dim(gathered, g ^ group, 0, False), g * depth, 0)
            for g in range(groups)
        ]
    else:
        pieces = [
            (a, (owner % groups ^ group) * depth + first, owner // groups * a.shape[1])
            for a, owner, first in gather_pieces(out_piece, n)
        ]
    return output(blocks, pieces)


def solution(mesh):
    in_specs = (
        P("seq", None),
        P("seq", "head"),
        P("seq", "head"),
        P("seq", "head"),
        P("head", "seq"),
        P("head", None, "seq"),
    )
    out_specs = P("seq", "head")
    return jax.shard_map(
        per_device, mesh=mesh, in_specs=in_specs, out_specs=out_specs, check_vma=False
    )
```

```python
import functools

import jax
import jax.numpy as jnp
from jax import lax
from jax.experimental import pallas as pl
from jax.experimental.pallas import tpu as pltpu
from jax.sharding import PartitionSpec as P

F32, BF16 = jnp.float32, jnp.bfloat16
LONGEST_RING = 16
SLOWER = 4
VMEM_BYTES = 56 * 2**20
VMEM = pl.BlockSpec(memory_space=pltpu.VMEM)
HBM = pl.BlockSpec(memory_space=pl.ANY)
WHOLE = lambda shape: pl.BlockSpec(shape, lambda *_: (0,) * len(shape))
SMEM = pl.BlockSpec(memory_space=pltpu.SMEM)


def call(kernel, outs, operands, scratch=(), **grid):
    nbytes = sum(a.size * a.dtype.itemsize for a in (*operands, *outs))
    return pl.pallas_call(
        kernel,
        out_shape=outs,
        scratch_shapes=list(scratch),
        compiler_params=pltpu.CompilerParams(vmem_limit_bytes=VMEM_BYTES),
        cost_estimate=pl.CostEstimate(
            flops=1, bytes_accessed=SLOWER * nbytes, transcendentals=0
        ),
        **grid,
    )(*operands)


def ring_order(n):
    return list(range(0, n, 2)) + list(range(n - 1, 0, -2))


def ring_position(index, n):
    return jnp.where(index % 2 == 0, index // 2, n - 1 - index // 2)


def ring_owner(position, n):
    position = (position + n) % n
    return jnp.where(position < n // 2, 2 * position, 2 * (n - 1 - position) + 1)


class Ring:
    def __init__(self, piece, n, opposite):
        order = ring_order(n)
        self.n, self.opposite, self.step = n, opposite, 0
        self.onward = [(order[i], order[(i + 1) % n]) for i in range(n)]
        self.back = [(b, a) for a, b in self.onward]
        self.here = ring_position(lax.axis_index("seq"), n)
        self.ways = [piece, piece]
        self.pieces = [(piece, lax.axis_index("seq"))]
        self.gate = ()

    def advance(self, *gate):
        self.step += 1
        self.gate = tuple(self.ways)
        last = self.step == self.n // 2
        for way, pairs in enumerate((self.onward, self.back)):
            if last and self.opposite != way:
                continue
            piece = self.ways[way]
            self.ways[way] = lax.ppermute(after(piece, gate), "seq", pairs)
            owner = ring_owner(self.here + (self.step if way else -self.step), self.n)
            self.pieces.append((self.ways[way], owner))


def after(array, others):
    return lax.optimization_barrier((array, *others))[0] if others else array


def copy_all(copies):
    for copy in copies:
        copy.start()
    return copies


def fetch(pieces, starts, whole, sems, cols=None):
    copies = []
    for i, piece in enumerate(pieces):
        piece = piece if cols is None else piece.at[:, cols]
        rows, width = piece.shape
        down = pl.ds(pl.multiple_of(starts[0, i], rows), rows)
        along = pl.ds(pl.multiple_of(starts[1, i], width), width)
        copies.append(pltpu.make_async_copy(piece, whole.at[down, along], sems.at[i]))
    return copy_all(copies)


def table(starts):
    return jnp.stack([jnp.stack([jnp.asarray(p[i], jnp.int32) for p in starts]) for i in (0, 1)])


def wait_all(copies):
    for copy in copies:
        copy.wait()


def multiply(left, right, out):
    width = min(256, out.shape[1])
    for low in range(0, out.shape[1], width):
        cols = slice(low, low + width)
        out[:, cols] = jnp.dot(left[...], right[:, cols], preferred_element_type=F32).astype(BF16)


def semaphores(*counts):
    return [pltpu.SemaphoreType.DMA((count,)) for count in counts]


def fetch_rows(array, local, sems):
    rows = local.shape[0] // sems.shape[0]
    parts = [slice(i * rows, (i + 1) * rows) for i in range(sems.shape[0])]
    return copy_all(
        [pltpu.make_async_copy(array.at[p], local.at[p], sems.at[i]) for i, p in enumerate(parts)]
    )


def local_kernel(count, starts, tokens, mixing, *refs):
    key_pieces, value_pieces, query_pieces = [
        refs[i * count : (i + 1) * count] for i in range(3)
    ]
    queries, local, states, rounded, *refs = refs[3 * count :]
    own_tokens, *wholes, keys, values, own_mixing, token_sems, mixing_sems, sems = refs
    rows, width = queries.shape
    heads, dim = states.shape[:2]
    copies = fetch_rows(tokens, own_tokens, token_sems)
    copies += fetch(key_pieces, starts, wholes[0], sems.at[0])
    wait_all(copies)
    copies = fetch(value_pieces, starts, wholes[1], sems.at[1])
    multiply(own_tokens, wholes[0], keys)
    wait_all(copies)
    copies = fetch(query_pieces, starts, wholes[2], sems.at[2])
    copies += fetch_rows(mixing, own_mixing, mixing_sems)
    multiply(own_tokens, wholes[1], values)
    for head in range(heads):
        own = slice(head * dim, (head + 1) * dim)
        sums = lax.dot_general(
            keys[:, own], values[:, own], (((0,), (0,)), ((), ())), preferred_element_type=F32
        )
        states[head] = sums
        rounded[head] = sums.astype(BF16)
    wait_all(copies)
    multiply(own_tokens, wholes[2], queries)
    tile = min(256, rows)
    for head in range(heads):
        own = slice(head * dim, (head + 1) * dim)
        for low in range(0, rows, tile):
            span, seen = slice(low, low + tile), slice(0, low + tile)
            scores = lax.dot_general(
                queries[span, own],
                keys[seen, own],
                (((1,), (1,)), ((), ())),
                preferred_element_type=F32,
            )
            mixed = (scores * own_mixing[head, span, seen].astype(F32)).astype(BF16)
            local[span, own] = jnp.dot(mixed, values[seen, own], preferred_element_type=F32)


def attend_locally(tokens, starts, key_pieces, value_pieces, query_pieces, mixing):
    arrays = [*key_pieces, *value_pieces, *query_pieces]
    count = len(key_pieces)
    rows, depth = tokens.shape
    width = arrays[0].shape[1]
    heads = mixing.shape[0]
    dim = width // heads
    shapes = [(rows, width)] * 2 + [(heads, dim, dim)] * 2
    return call(
        functools.partial(local_kernel, count),
        [jax.ShapeDtypeStruct(s, t) for s, t in zip(shapes, (BF16, F32, F32, BF16))],
        [starts, tokens, mixing, *arrays],
        [
            pltpu.VMEM((rows, depth), BF16),
            *[pltpu.VMEM((depth, width), BF16)] * 3,
            *[pltpu.VMEM((rows, width), BF16)] * 2,
            pltpu.VMEM(mixing.shape, BF16),
            *semaphores(8, heads),
            pltpu.SemaphoreType.DMA((3, count)),
        ],
        in_specs=[SMEM] + [HBM] * (2 + len(arrays)),
        out_specs=[WHOLE(s) for s in shapes],
        grid=(1,),
    )


def mixing_kernel(bits, weights, mixing):
    rows = mixing.shape[1]
    tile = min(256, rows)
    tile_bits = tile.bit_length() - 1
    column = lambda level, low: weights[0, low : low + tile, level : level + 1]
    t = lax.broadcasted_iota(jnp.int32, (tile, tile), 0)
    s = lax.broadcasted_iota(jnp.int32, (tile, tile), 1)
    apart = jnp.bitwise_xor(t, s)
    for low in range(0, rows, tile):
        for left in range(0, low, tile):
            level = tile_bits + ((low // tile) ^ (left // tile)).bit_length()
            mixing[0, low : low + tile, left : left + tile] = jnp.broadcast_to(
                column(level, low), (tile, tile)
            ).astype(BF16)
        mixed = jnp.broadcast_to(column(0, low), (tile, tile))
        for level in range(1, tile_bits + 1):
            mixed = jnp.where(apart >= 1 << (level - 1), column(level, low), mixed)
        mixing[0, low : low + tile, low : low + tile] = jnp.where(s <= t, mixed, 0.0).astype(BF16)


def mixing_matrix(weights_by_token, bits):
    heads, rows, levels = weights_by_token.shape
    return call(
        functools.partial(mixing_kernel, bits),
        [jax.ShapeDtypeStruct((heads, rows, rows), BF16)],
        [weights_by_token],
        grid=(heads,),
        in_specs=[pl.BlockSpec((1, rows, levels), lambda h: (h, 0, 0))],
        out_specs=[pl.BlockSpec((1, rows, rows), lambda h: (h, 0, 0))],
    )[0]


def fetch_columns(pieces, starts, low, whole, sems, act):
    for i, piece in enumerate(pieces):
        column = starts[1, i] - low

        @pl.when((column >= 0) & (column < whole.shape[1]))
        def _():
            along = pl.ds(pl.multiple_of(column, piece.shape[1]), piece.shape[1])
            getattr(pltpu.make_async_copy(piece, whole.at[:, along], sems.at[i]), act)()


def multiply_groups(attended, whole, outs):
    width = outs[0].shape[1]
    for i, out in reversed(list(enumerate(outs))):
        cols = slice(i * width, (i + 1) * width)
        out[...] = jnp.dot(
            attended[...], whole[:, cols], preferred_element_type=F32
        ).astype(BF16)


def finish_kernel(count, terms_count, upper, starts, queries, local, weights, *refs):
    pieces, terms, refs = refs[:count], refs[count : count + terms_count], refs[count + terms_count :]
    attended, *outs = refs[:-7]
    query, sums, own_weights, own_terms, whole, sems, piece_sems = refs[-7:]
    columns = whole.shape[1]
    copies = copy_all(
        [
            pltpu.make_async_copy(array, scratch, sems.at[i])
            for i, (array, scratch) in enumerate(
                [(queries, query), (local, sums), (weights, own_weights)]
                + [(term, own_terms.at[i]) for i, term in enumerate(terms)]
            )
        ]
    )
    fetch_columns(pieces, starts, columns, whole, piece_sems, "start")
    wait_all(copies)
    heads, dim = own_terms.shape[1:3]
    first = own_weights.shape[2] - upper.shape[0]
    rows = query.shape[0]
    tile = min(256, rows)
    for low in range(0, rows, tile):
        span = slice(low, low + tile)
        for head in range(heads):
            own = slice(head * dim, (head + 1) * dim)
            total = sums[span, own]
            for i in range(terms_count):
                level = i if i < 2 else i - 1
                weight = own_weights[head, span, first + level : first + level + 1]
                total += (weight * upper[level]) * jnp.dot(
                    query[span, own], own_terms[i, head], preferred_element_type=F32
                )
            scale = lax.rsqrt(jnp.mean(total * total, axis=-1, keepdims=True) + 1e-06)
            attended[span, own] = (total * scale).astype(BF16)
    fetch_columns(pieces, starts, columns, whole, piece_sems, "wait")
    multiply_groups(attended, whole, outs)


def finish(queries, local, weights, upper, terms, starts, pieces, groups):
    rows, inner = queries.shape
    width = sum(a.size for a in pieces) // inner // groups
    count = groups // 2
    return call(
        functools.partial(finish_kernel, len(pieces), len(terms)),
        [jax.ShapeDtypeStruct(queries.shape, BF16)]
        + [jax.ShapeDtypeStruct((rows, width), BF16)] * count,
        [upper, starts, queries, local, weights, *pieces, *terms],
        [
            pltpu.VMEM(queries.shape, BF16),
            pltpu.VMEM(local.shape, F32),
            pltpu.VMEM(weights.shape, F32),
            pltpu.VMEM((len(terms), *terms[0].shape), BF16),
            pltpu.VMEM((inner, width * count), BF16),
            *semaphores(3 + len(terms), len(pieces)),
        ],
        in_specs=[SMEM] * 2 + [HBM] * (3 + len(pieces) + len(terms)),
        out_specs=[WHOLE(queries.shape)] + [WHOLE((rows, width))] * count,
        grid=(1,),
    )


def output_kernel(count, starts, attended, *refs):
    pieces, (*outs, whole, sems) = refs[:count], refs[count:]
    for act in ("start", "wait"):
        fetch_columns(pieces, starts, 0, whole, sems, act)
    multiply_groups(attended, whole, outs)


def output(attended, starts, pieces, groups):
    rows, inner = attended.shape
    width = sum(a.size for a in pieces) // inner // groups
    count = groups // 2
    return call(
        functools.partial(output_kernel, len(pieces)),
        [jax.ShapeDtypeStruct((rows, width), BF16)] * count,
        [starts, attended, *pieces],
        [pltpu.VMEM((inner, width * count), BF16), *semaphores(len(pieces))],
        in_specs=[SMEM, WHOLE((rows, inner))] + [HBM] * len(pieces),
        out_specs=[WHOLE((rows, width))] * count,
        grid=(1,),
    )


def per_device(tokens, w_query, w_key, w_value, w_out, level_weights):
    n = lax.axis_size("seq")
    groups = lax.axis_size("head")
    here = lax.axis_index("seq")
    group = lax.axis_index("head")
    local_bits = tokens.shape[0].bit_length() - 1
    heads = level_weights.shape[0]
    ringed = n <= LONGEST_RING and n % 2 == 0

    share = n // groups
    depth, width = w_query.shape[0], w_out.shape[1]
    bits = n.bit_length() - 1
    upper = jnp.stack([here >> bit & 1 for bit in range(bits)]).astype(F32)
    weights_by_token = level_weights.transpose(0, 2, 1)
    if ringed:
        key, value, query, out = [
            Ring(w, n, i % 2) for i, w in enumerate((w_key, w_value, w_query, w_out))
        ]
        mixing = mixing_matrix(weights_by_token, local_bits)
        for step in range(1, n // 2 + 1):
            key.advance(*((mixing,) if step == 3 else ()))
            value.advance()
            query.advance()
            if step > 1:
                out.advance(*(key.gate if step == 2 else ()))
        pieces = [[a for a, _ in ring.pieces] for ring in (key, value, query)]
        starts = table([(owner * depth, 0) for _, owner in key.pieces])
    else:
        mixing = mixing_matrix(weights_by_token, local_bits)
        pieces = [
            [lax.all_gather(w, "seq", axis=0, tiled=True)] for w in (w_key, w_value, w_query)
        ]
        starts = table([(0, 0)])
    queries, local, running, rounded = attend_locally(tokens, starts, *pieces, mixing)

    def from_partner(array, apart):
        return lax.ppermute(array, "seq", [(i, i ^ apart) for i in range(n)])

    terms = [from_partner(rounded, apart) for apart in (1, 2, 3)]
    for bit in range(2, bits):
        for term in terms[-3:] if bit == 2 else terms[-1:]:
            running = running + term.astype(F32)
        terms = terms + [from_partner(running.astype(BF16), 1 << bit)]
    if ringed:
        out.advance(rounded)
        out_pieces = [a for a, _ in out.pieces]
        out_starts = [
            (0, ((owner // share ^ group) * share + owner % share) * width)
            for _, owner in out.pieces
        ]
    else:
        whole = lax.all_gather(w_out, "seq", axis=1, tiled=True)
        width *= share
        out_pieces = [
            lax.dynamic_slice_in_dim(whole, (group ^ k) * width, width, 1) for k in range(groups)
        ]
        out_starts = [(0, k * width) for k in range(groups)]

    far = groups.bit_length() - 2

    def from_group(array, bit):
        return lax.ppermute(array, "head", [(g, g ^ 1 << bit) for g in range(groups)])

    def sum_near(shares, kind):
        for bit in range(far):
            theirs = {k ^ 1 << bit: from_group(a, bit) for k, a in shares.items() if k >> bit & 1}
            shares = {
                k: (shares[k].astype(F32) + a.astype(F32)).astype(kind) for k, a in theirs.items()
            }
        (total,) = shares.values()
        return total

    starts = table(out_starts)
    attended, *shares = finish(
        queries, local, weights_by_token, upper, terms, starts, out_pieces, groups
    )
    away = sum_near({groups // 2 + k: a for k, a in enumerate(shares)}, BF16)
    theirs = from_group(away, far)
    shares = output(after(attended, [away]), starts, out_pieces, groups)
    ours = sum_near(dict(enumerate(shares)), F32)
    return (ours.astype(F32) + theirs.astype(F32)).astype(BF16)


def solution(mesh):
    in_specs = (
        P("seq", None),
        P("seq", "head"),
        P("seq", "head"),
        P("seq", "head"),
        P("head", "seq"),
        P("head", None, "seq"),
    )
    out_specs = P("seq", "head")
    return jax.shard_map(
        per_device, mesh=mesh, in_specs=in_specs, out_specs=out_specs, check_vma=False
    )
```

```python
import functools

import jax
import jax.numpy as jnp
from jax import lax
from jax.experimental import pallas as pl
from jax.experimental.pallas import tpu as pltpu
from jax.sharding import PartitionSpec as P

F32, BF16 = jnp.float32, jnp.bfloat16
LONGEST_RING = 16
SLOWER = 4
VMEM_BYTES = 56 * 2**20
VMEM = pl.BlockSpec(memory_space=pltpu.VMEM)
HBM = pl.BlockSpec(memory_space=pl.ANY)
WHOLE = lambda shape: pl.BlockSpec(shape, lambda *_: (0,) * len(shape))
SMEM = pl.BlockSpec(memory_space=pltpu.SMEM)


def call(kernel, outs, operands, scratch=(), **grid):
    nbytes = sum(a.size * a.dtype.itemsize for a in (*operands, *outs))
    return pl.pallas_call(
        kernel,
        out_shape=outs,
        scratch_shapes=list(scratch),
        compiler_params=pltpu.CompilerParams(vmem_limit_bytes=VMEM_BYTES),
        cost_estimate=pl.CostEstimate(
            flops=1, bytes_accessed=SLOWER * nbytes, transcendentals=0
        ),
        **grid,
    )(*operands)


def ring_order(n):
    return list(range(0, n, 2)) + list(range(n - 1, 0, -2))


def ring_position(index, n):
    return jnp.where(index % 2 == 0, index // 2, n - 1 - index // 2)


def ring_owner(position, n):
    position = (position + n) % n
    return jnp.where(position < n // 2, 2 * position, 2 * (n - 1 - position) + 1)


class Ring:
    def __init__(self, piece, n, opposite):
        order = ring_order(n)
        self.n, self.opposite, self.step = n, opposite, 0
        self.onward = [(order[i], order[(i + 1) % n]) for i in range(n)]
        self.back = [(b, a) for a, b in self.onward]
        self.here = ring_position(lax.axis_index("seq"), n)
        self.ways = [piece, piece]
        self.pieces = [(piece, lax.axis_index("seq"))]
        self.gate = ()

    def advance(self, *gate):
        self.step += 1
        self.gate = tuple(self.ways)
        last = self.step == self.n // 2
        for way, pairs in enumerate((self.onward, self.back)):
            if last and self.opposite != way:
                continue
            piece = self.ways[way]
            self.ways[way] = lax.ppermute(after(piece, gate), "seq", pairs)
            owner = ring_owner(self.here + (self.step if way else -self.step), self.n)
            self.pieces.append((self.ways[way], owner))


def after(array, others):
    return lax.optimization_barrier((array, *others))[0] if others else array


def copy_all(copies):
    for copy in copies:
        copy.start()
    return copies


def fetch(pieces, starts, whole, sems, cols=None):
    copies = []
    for i, piece in enumerate(pieces):
        piece = piece if cols is None else piece.at[:, cols]
        rows, width = piece.shape
        down = pl.ds(pl.multiple_of(starts[0, i], rows), rows)
        along = pl.ds(pl.multiple_of(starts[1, i], width), width)
        copies.append(pltpu.make_async_copy(piece, whole.at[down, along], sems.at[i]))
    return copy_all(copies)


def table(starts):
    return jnp.stack([jnp.stack([jnp.asarray(p[i], jnp.int32) for p in starts]) for i in (0, 1)])


def wait_all(copies):
    for copy in copies:
        copy.wait()


def multiply(left, right, out):
    width = min(256, out.shape[1])
    for low in range(0, out.shape[1], width):
        cols = slice(low, low + width)
        out[:, cols] = jnp.dot(left[...], right[:, cols], preferred_element_type=F32).astype(BF16)


def semaphores(*counts):
    return [pltpu.SemaphoreType.DMA((count,)) for count in counts]


def fetch_rows(array, local, sems):
    rows = local.shape[0] // sems.shape[0]
    parts = [slice(i * rows, (i + 1) * rows) for i in range(sems.shape[0])]
    return copy_all(
        [pltpu.make_async_copy(array.at[p], local.at[p], sems.at[i]) for i, p in enumerate(parts)]
    )


def key_value_kernel(count, starts, tokens, *refs):
    key_pieces, value_pieces, refs = refs[:count], refs[count : 2 * count], refs[2 * count :]
    keys, values, states, rounded, own_tokens, whole, whole_values, token_sems, sems = refs
    copies = fetch_rows(tokens, own_tokens, token_sems)
    wait_all(copies + fetch(key_pieces, starts, whole, sems.at[0]))
    copies = fetch(value_pieces, starts, whole_values, sems.at[1])
    multiply(own_tokens, whole, keys)
    wait_all(copies)
    multiply(own_tokens, whole_values, values)
    heads, dim = states.shape[:2]
    for head in range(heads):
        own = slice(head * dim, (head + 1) * dim)
        sums = lax.dot_general(
            keys[:, own], values[:, own], (((0,), (0,)), ((), ())), preferred_element_type=F32
        )
        states[head] = sums
        rounded[head] = sums.astype(BF16)


def project_keys_values(tokens, starts, key_pieces, value_pieces, heads):
    arrays = [*key_pieces, *value_pieces]
    count = len(key_pieces)
    rows, depth = tokens.shape
    width = arrays[0].shape[1]
    dim = width // heads
    shapes = [(rows, width)] * 2 + [(heads, dim, dim)] * 2
    return call(
        functools.partial(key_value_kernel, count),
        [jax.ShapeDtypeStruct(s, t) for s, t in zip(shapes, (BF16, BF16, F32, BF16))],
        [starts, tokens, *arrays],
        [
            pltpu.VMEM((rows, depth), BF16),
            *[pltpu.VMEM((depth, width), BF16)] * 2,
            *semaphores(8),
            pltpu.SemaphoreType.DMA((2, count)),
        ],
        in_specs=[SMEM] + [HBM] * (1 + len(arrays)),
        out_specs=[WHOLE(s) for s in shapes],
        grid=(1,),
    )


def local_kernel(starts, tokens, keys, values, mixing, *refs):
    *pieces, queries, local, own_tokens, whole, key, value, mix, token_sems, mix_sems, sems, more = refs
    copies = fetch_rows(tokens, own_tokens, token_sems)
    copies += fetch(pieces, starts, whole, sems)
    wait_all(copies)
    copies = fetch_rows(mixing, mix, mix_sems)
    copies += copy_all(
        [
            pltpu.make_async_copy(keys, key, more.at[0]),
            pltpu.make_async_copy(values, value, more.at[1]),
        ]
    )
    multiply(own_tokens, whole, queries)
    wait_all(copies)
    rows = queries.shape[0]
    heads = mix.shape[0]
    dim = queries.shape[1] // heads
    tile = min(256, rows)
    for head in range(heads):
        own = slice(head * dim, (head + 1) * dim)
        for low in range(0, rows, tile):
            span, seen = slice(low, low + tile), slice(0, low + tile)
            scores = lax.dot_general(
                queries[span, own],
                key[seen, own],
                (((1,), (1,)), ((), ())),
                preferred_element_type=F32,
            )
            mixed = (scores * mix[head, span, seen].astype(F32)).astype(BF16)
            local[span, own] = jnp.dot(mixed, value[seen, own], preferred_element_type=F32)


def attend_locally(tokens, starts, pieces, keys, values, mixing):
    rows, depth = tokens.shape
    shape = keys.shape
    return call(
        local_kernel,
        [jax.ShapeDtypeStruct(shape, BF16), jax.ShapeDtypeStruct(shape, F32)],
        [starts, tokens, keys, values, mixing, *pieces],
        [
            pltpu.VMEM((rows, depth), BF16),
            pltpu.VMEM((depth, shape[1]), BF16),
            *[pltpu.VMEM(shape, BF16)] * 2,
            pltpu.VMEM(mixing.shape, BF16),
            *semaphores(8, mixing.shape[0], len(pieces), 2),
        ],
        in_specs=[SMEM] + [HBM] * (4 + len(pieces)),
        out_specs=[WHOLE(shape)] * 2,
        grid=(1,),
    )


def mixing_kernel(bits, weights, mixing):
    rows = mixing.shape[1]
    tile = min(256, rows)
    tile_bits = tile.bit_length() - 1
    column = lambda level, low: weights[0, low : low + tile, level : level + 1]
    t = lax.broadcasted_iota(jnp.int32, (tile, tile), 0)
    s = lax.broadcasted_iota(jnp.int32, (tile, tile), 1)
    apart = jnp.bitwise_xor(t, s)
    for low in range(0, rows, tile):
        for left in range(0, low, tile):
            level = tile_bits + ((low // tile) ^ (left // tile)).bit_length()
            mixing[0, low : low + tile, left : left + tile] = jnp.broadcast_to(
                column(level, low), (tile, tile)
            ).astype(BF16)
        mixed = jnp.broadcast_to(column(0, low), (tile, tile))
        for level in range(1, tile_bits + 1):
            mixed = jnp.where(apart >= 1 << (level - 1), column(level, low), mixed)
        mixing[0, low : low + tile, low : low + tile] = jnp.where(s <= t, mixed, 0.0).astype(BF16)


def mixing_matrix(weights_by_token, bits):
    heads, rows, levels = weights_by_token.shape
    return call(
        functools.partial(mixing_kernel, bits),
        [jax.ShapeDtypeStruct((heads, rows, rows), BF16)],
        [weights_by_token],
        grid=(heads,),
        in_specs=[pl.BlockSpec((1, rows, levels), lambda h: (h, 0, 0))],
        out_specs=[pl.BlockSpec((1, rows, rows), lambda h: (h, 0, 0))],
    )[0]


def fetch_columns(pieces, starts, low, whole, sems, act):
    for i, piece in enumerate(pieces):
        column = starts[1, i] - low

        @pl.when((column >= 0) & (column < whole.shape[1]))
        def _():
            along = pl.ds(pl.multiple_of(column, piece.shape[1]), piece.shape[1])
            getattr(pltpu.make_async_copy(piece, whole.at[:, along], sems.at[i]), act)()


def multiply_groups(attended, whole, outs):
    width = outs[0].shape[1]
    for i, out in reversed(list(enumerate(outs))):
        cols = slice(i * width, (i + 1) * width)
        out[...] = jnp.dot(
            attended[...], whole[:, cols], preferred_element_type=F32
        ).astype(BF16)


def finish_kernel(count, terms_count, upper, starts, queries, local, weights, *refs):
    pieces, terms, refs = refs[:count], refs[count : count + terms_count], refs[count + terms_count :]
    attended, *outs = refs[:-7]
    query, sums, own_weights, own_terms, whole, sems, piece_sems = refs[-7:]
    columns = whole.shape[1]
    copies = copy_all(
        [
            pltpu.make_async_copy(array, scratch, sems.at[i])
            for i, (array, scratch) in enumerate(
                [(queries, query), (local, sums), (weights, own_weights)]
                + [(term, own_terms.at[i]) for i, term in enumerate(terms)]
            )
        ]
    )
    fetch_columns(pieces, starts, columns, whole, piece_sems, "start")
    wait_all(copies)
    heads, dim = own_terms.shape[1:3]
    first = own_weights.shape[2] - upper.shape[0]
    rows = query.shape[0]
    tile = min(256, rows)
    for low in range(0, rows, tile):
        span = slice(low, low + tile)
        for head in range(heads):
            own = slice(head * dim, (head + 1) * dim)
            total = sums[span, own]
            for i in range(terms_count):
                level = i if i < 2 else i - 1
                weight = own_weights[head, span, first + level : first + level + 1]
                total += (weight * upper[level]) * jnp.dot(
                    query[span, own], own_terms[i, head], preferred_element_type=F32
                )
            scale = lax.rsqrt(jnp.mean(total * total, axis=-1, keepdims=True) + 1e-06)
            attended[span, own] = (total * scale).astype(BF16)
    fetch_columns(pieces, starts, columns, whole, piece_sems, "wait")
    multiply_groups(attended, whole, outs)


def finish(queries, local, weights, upper, terms, starts, pieces, groups):
    rows, inner = queries.shape
    width = sum(a.size for a in pieces) // inner // groups
    count = groups // 2
    return call(
        functools.partial(finish_kernel, len(pieces), len(terms)),
        [jax.ShapeDtypeStruct(queries.shape, BF16)]
        + [jax.ShapeDtypeStruct((rows, width), BF16)] * count,
        [upper, starts, queries, local, weights, *pieces, *terms],
        [
            pltpu.VMEM(queries.shape, BF16),
            pltpu.VMEM(local.shape, F32),
            pltpu.VMEM(weights.shape, F32),
            pltpu.VMEM((len(terms), *terms[0].shape), BF16),
            pltpu.VMEM((inner, width * count), BF16),
            *semaphores(3 + len(terms), len(pieces)),
        ],
        in_specs=[SMEM] * 2 + [HBM] * (3 + len(pieces) + len(terms)),
        out_specs=[WHOLE(queries.shape)] + [WHOLE((rows, width))] * count,
        grid=(1,),
    )


def output_kernel(count, starts, attended, *refs):
    pieces, (*outs, whole, sems) = refs[:count], refs[count:]
    for act in ("start", "wait"):
        fetch_columns(pieces, starts, 0, whole, sems, act)
    multiply_groups(attended, whole, outs)


def output(attended, starts, pieces, groups):
    rows, inner = attended.shape
    width = sum(a.size for a in pieces) // inner // groups
    count = groups // 2
    return call(
        functools.partial(output_kernel, len(pieces)),
        [jax.ShapeDtypeStruct((rows, width), BF16)] * count,
        [starts, attended, *pieces],
        [pltpu.VMEM((inner, width * count), BF16), *semaphores(len(pieces))],
        in_specs=[SMEM, WHOLE((rows, inner))] + [HBM] * len(pieces),
        out_specs=[WHOLE((rows, width))] * count,
        grid=(1,),
    )


def per_device(tokens, w_query, w_key, w_value, w_out, level_weights):
    n = lax.axis_size("seq")
    groups = lax.axis_size("head")
    here = lax.axis_index("seq")
    group = lax.axis_index("head")
    local_bits = tokens.shape[0].bit_length() - 1
    heads = level_weights.shape[0]
    ringed = n <= LONGEST_RING and n % 2 == 0

    share = n // groups
    depth, width = w_query.shape[0], w_out.shape[1]
    bits = n.bit_length() - 1
    upper = jnp.stack([here >> bit & 1 for bit in range(bits)]).astype(F32)
    weights_by_token = level_weights.transpose(0, 2, 1)
    if ringed:
        key, value, query, out = [
            Ring(w, n, i % 2) for i, w in enumerate((w_key, w_value, w_query, w_out))
        ]
        mixing = mixing_matrix(weights_by_token, local_bits)
        for step in range(1, n // 2 + 1):
            key.advance(*((mixing,) if step == 3 else ()))
            value.advance()
            query.advance()
            if step > 1:
                out.advance(*(key.gate if step == 2 else ()))
        pieces = [[a for a, _ in ring.pieces] for ring in (key, value, query)]
        starts = table([(owner * depth, 0) for _, owner in key.pieces])
    else:
        mixing = mixing_matrix(weights_by_token, local_bits)
        pieces = [
            [lax.all_gather(w, "seq", axis=0, tiled=True)] for w in (w_key, w_value, w_query)
        ]
        starts = table([(0, 0)])
    *pieces, query_pieces = pieces
    keys, values, running, rounded = project_keys_values(tokens, starts, *pieces, heads)

    def from_partner(array, apart):
        return lax.ppermute(array, "seq", [(i, i ^ apart) for i in range(n)])

    terms = [from_partner(rounded, apart) for apart in (1, 2, 3)]
    for bit in range(2, bits):
        for term in terms[-3:] if bit == 2 else terms[-1:]:
            running = running + term.astype(F32)
        terms = terms + [from_partner(running.astype(BF16), 1 << bit)]
    tokens = after(tokens, [running])
    queries, local = attend_locally(tokens, starts, query_pieces, keys, values, mixing)
    if ringed:
        out.advance(rounded)
        out_pieces = [a for a, _ in out.pieces]
        out_starts = [
            (0, ((owner // share ^ group) * share + owner % share) * width)
            for _, owner in out.pieces
        ]
    else:
        whole = lax.all_gather(w_out, "seq", axis=1, tiled=True)
        width *= share
        out_pieces = [
            lax.dynamic_slice_in_dim(whole, (group ^ k) * width, width, 1) for k in range(groups)
        ]
        out_starts = [(0, k * width) for k in range(groups)]

    far = groups.bit_length() - 2

    def from_group(array, bit):
        return lax.ppermute(array, "head", [(g, g ^ 1 << bit) for g in range(groups)])

    def sum_near(shares, kind):
        for bit in range(far):
            theirs = {k ^ 1 << bit: from_group(a, bit) for k, a in shares.items() if k >> bit & 1}
            shares = {
                k: (shares[k].astype(F32) + a.astype(F32)).astype(kind) for k, a in theirs.items()
            }
        (total,) = shares.values()
        return total

    starts = table(out_starts)
    attended, *shares = finish(
        queries, local, weights_by_token, upper, terms, starts, out_pieces, groups
    )
    away = sum_near({groups // 2 + k: a for k, a in enumerate(shares)}, BF16)
    theirs = from_group(away, far)
    shares = output(after(attended, [away]), starts, out_pieces, groups)
    ours = sum_near(dict(enumerate(shares)), F32)
    return (ours.astype(F32) + theirs.astype(F32)).astype(BF16)


def solution(mesh):
    in_specs = (
        P("seq", None),
        P("seq", "head"),
        P("seq", "head"),
        P("seq", "head"),
        P("head", "seq"),
        P("head", None, "seq"),
    )
    out_specs = P("seq", "head")
    return jax.shard_map(
        per_device, mesh=mesh, in_specs=in_specs, out_specs=out_specs, check_vma=False
    )
```

```python
import functools

import jax
import jax.numpy as jnp
from jax import lax
from jax.experimental import pallas as pl
from jax.experimental.pallas import tpu as pltpu
from jax.sharding import PartitionSpec as P

F32, BF16 = jnp.float32, jnp.bfloat16
LONGEST_RING = 16
SLOWER = 4
VMEM_BYTES = 56 * 2**20
VMEM = pl.BlockSpec(memory_space=pltpu.VMEM)
HBM = pl.BlockSpec(memory_space=pl.ANY)
WHOLE = lambda shape: pl.BlockSpec(shape, lambda *_: (0,) * len(shape))
SMEM = pl.BlockSpec(memory_space=pltpu.SMEM)


def call(kernel, outs, operands, scratch=(), **grid):
    nbytes = sum(a.size * a.dtype.itemsize for a in (*operands, *outs))
    return pl.pallas_call(
        kernel,
        out_shape=outs,
        scratch_shapes=list(scratch),
        compiler_params=pltpu.CompilerParams(vmem_limit_bytes=VMEM_BYTES),
        cost_estimate=pl.CostEstimate(
            flops=1, bytes_accessed=SLOWER * nbytes, transcendentals=0
        ),
        **grid,
    )(*operands)


def ring_order(n):
    return list(range(0, n, 2)) + list(range(n - 1, 0, -2))


def ring_position(index, n):
    return jnp.where(index % 2 == 0, index // 2, n - 1 - index // 2)


def ring_owner(position, n):
    position = (position + n) % n
    return jnp.where(position < n // 2, 2 * position, 2 * (n - 1 - position) + 1)


def piece_owners(n):
    here = ring_position(lax.axis_index("seq"), n)
    owners = [lax.axis_index("seq")]
    for step in range(1, n // 2):
        owners += [ring_owner(here - step, n), ring_owner(here + step, n)]
    return owners + [ring_owner(here + n // 2, n)]


class Ring:
    def __init__(self, piece, n, opposite):
        order = ring_order(n)
        self.n, self.opposite, self.step = n, opposite, 0
        self.onward = [(order[i], order[(i + 1) % n]) for i in range(n)]
        self.back = [(b, a) for a, b in self.onward]
        self.ways = [piece, piece]
        self.pieces = [piece]
        self.gate = ()

    def advance(self, *gate):
        self.step += 1
        self.gate = tuple(self.ways)
        last = self.step == self.n // 2
        for way, pairs in enumerate((self.onward, self.back)):
            if last and self.opposite != way:
                continue
            piece = self.ways[way]
            self.ways[way] = lax.ppermute(after(piece, gate), "seq", pairs)
            self.pieces.append(self.ways[way])


def after(array, others):
    return lax.optimization_barrier((array, *others))[0] if others else array


def copy_all(copies):
    for copy in copies:
        copy.start()
    return copies


def fetch(pieces, starts, whole, sems, cols=None):
    copies = []
    for i, piece in enumerate(pieces):
        piece = piece if cols is None else piece.at[:, cols]
        rows, width = piece.shape
        down = pl.ds(pl.multiple_of(starts[0, i], rows), rows)
        along = pl.ds(pl.multiple_of(starts[1, i], width), width)
        copies.append(pltpu.make_async_copy(piece, whole.at[down, along], sems.at[i]))
    return copy_all(copies)


def table(starts):
    return jnp.stack([jnp.stack([jnp.asarray(p[i], jnp.int32) for p in starts]) for i in (0, 1)])


def wait_all(copies):
    for copy in copies:
        copy.wait()


def multiply(left, right, out):
    width = min(256, out.shape[1])
    for low in range(0, out.shape[1], width):
        cols = slice(low, low + width)
        out[:, cols] = jnp.dot(left[...], right[:, cols], preferred_element_type=F32).astype(BF16)


def semaphores(*counts):
    return [pltpu.SemaphoreType.DMA((count,)) for count in counts]


def fetch_rows(array, local, sems):
    rows = local.shape[0] // sems.shape[0]
    parts = [slice(i * rows, (i + 1) * rows) for i in range(sems.shape[0])]
    return copy_all(
        [pltpu.make_async_copy(array.at[p], local.at[p], sems.at[i]) for i, p in enumerate(parts)]
    )


def key_value_kernel(count, starts, tokens, *refs):
    key_pieces, value_pieces, refs = refs[:count], refs[count : 2 * count], refs[2 * count :]
    keys, values, states, rounded, own_tokens, whole, whole_values, token_sems, sems = refs
    copies = fetch_rows(tokens, own_tokens, token_sems)
    wait_all(copies + fetch(key_pieces, starts, whole, sems.at[0]))
    copies = fetch(value_pieces, starts, whole_values, sems.at[1])
    multiply(own_tokens, whole, keys)
    wait_all(copies)
    multiply(own_tokens, whole_values, values)
    heads, dim = states.shape[:2]
    for head in range(heads):
        own = slice(head * dim, (head + 1) * dim)
        sums = lax.dot_general(
            keys[:, own], values[:, own], (((0,), (0,)), ((), ())), preferred_element_type=F32
        )
        states[head] = sums
        rounded[head] = sums.astype(BF16)


def project_keys_values(tokens, starts, key_pieces, value_pieces, heads):
    arrays = [*key_pieces, *value_pieces]
    count = len(key_pieces)
    rows, depth = tokens.shape
    width = arrays[0].shape[1]
    dim = width // heads
    shapes = [(rows, width)] * 2 + [(heads, dim, dim)] * 2
    return call(
        functools.partial(key_value_kernel, count),
        [jax.ShapeDtypeStruct(s, t) for s, t in zip(shapes, (BF16, BF16, F32, BF16))],
        [starts, tokens, *arrays],
        [
            pltpu.VMEM((rows, depth), BF16),
            *[pltpu.VMEM((depth, width), BF16)] * 2,
            *semaphores(8),
            pltpu.SemaphoreType.DMA((2, count)),
        ],
        in_specs=[SMEM] + [HBM] * (1 + len(arrays)),
        out_specs=[WHOLE(s) for s in shapes],
        grid=(1,),
    )


def local_kernel(starts, tokens, keys, values, mixing, *refs):
    *pieces, queries, local, own_tokens, whole, key, value, mix, token_sems, mix_sems, sems, more = refs
    copies = fetch_rows(tokens, own_tokens, token_sems)
    copies += fetch(pieces, starts, whole, sems)
    wait_all(copies)
    copies = fetch_rows(mixing, mix, mix_sems)
    copies += copy_all(
        [
            pltpu.make_async_copy(keys, key, more.at[0]),
            pltpu.make_async_copy(values, value, more.at[1]),
        ]
    )
    multiply(own_tokens, whole, queries)
    wait_all(copies)
    rows = queries.shape[0]
    heads = mix.shape[0]
    dim = queries.shape[1] // heads
    tile = min(256, rows)
    for head in range(heads):
        own = slice(head * dim, (head + 1) * dim)
        for low in range(0, rows, tile):
            span, seen = slice(low, low + tile), slice(0, low + tile)
            scores = lax.dot_general(
                queries[span, own],
                key[seen, own],
                (((1,), (1,)), ((), ())),
                preferred_element_type=F32,
            )
            mixed = (scores * mix[head, span, seen].astype(F32)).astype(BF16)
            local[span, own] = jnp.dot(mixed, value[seen, own], preferred_element_type=F32)


def attend_locally(tokens, starts, pieces, keys, values, mixing):
    rows, depth = tokens.shape
    shape = keys.shape
    return call(
        local_kernel,
        [jax.ShapeDtypeStruct(shape, BF16), jax.ShapeDtypeStruct(shape, F32)],
        [starts, tokens, keys, values, mixing, *pieces],
        [
            pltpu.VMEM((rows, depth), BF16),
            pltpu.VMEM((depth, shape[1]), BF16),
            *[pltpu.VMEM(shape, BF16)] * 2,
            pltpu.VMEM(mixing.shape, BF16),
            *semaphores(8, mixing.shape[0], len(pieces), 2),
        ],
        in_specs=[SMEM] + [HBM] * (4 + len(pieces)),
        out_specs=[WHOLE(shape)] * 2,
        grid=(1,),
    )


def mixing_kernel(bits, weights, mixing):
    rows = mixing.shape[1]
    tile = min(256, rows)
    tile_bits = tile.bit_length() - 1
    column = lambda level, low: weights[0, low : low + tile, level : level + 1]
    t = lax.broadcasted_iota(jnp.int32, (tile, tile), 0)
    s = lax.broadcasted_iota(jnp.int32, (tile, tile), 1)
    apart = jnp.bitwise_xor(t, s)
    for low in range(0, rows, tile):
        for left in range(0, low, tile):
            level = tile_bits + ((low // tile) ^ (left // tile)).bit_length()
            mixing[0, low : low + tile, left : left + tile] = jnp.broadcast_to(
                column(level, low), (tile, tile)
            ).astype(BF16)
        mixed = jnp.broadcast_to(column(0, low), (tile, tile))
        for level in range(1, tile_bits + 1):
            mixed = jnp.where(apart >= 1 << (level - 1), column(level, low), mixed)
        mixing[0, low : low + tile, low : low + tile] = jnp.where(s <= t, mixed, 0.0).astype(BF16)


def mixing_matrix(weights_by_token, bits):
    heads, rows, levels = weights_by_token.shape
    return call(
        functools.partial(mixing_kernel, bits),
        [jax.ShapeDtypeStruct((heads, rows, rows), BF16)],
        [weights_by_token],
        grid=(heads,),
        in_specs=[pl.BlockSpec((1, rows, levels), lambda h: (h, 0, 0))],
        out_specs=[pl.BlockSpec((1, rows, rows), lambda h: (h, 0, 0))],
    )[0]


def fetch_columns(pieces, starts, low, whole, sems, act):
    for i, piece in enumerate(pieces):
        column = starts[1, i] - low

        @pl.when((column >= 0) & (column < whole.shape[1]))
        def _():
            along = pl.ds(pl.multiple_of(column, piece.shape[1]), piece.shape[1])
            getattr(pltpu.make_async_copy(piece, whole.at[:, along], sems.at[i]), act)()


def multiply_groups(attended, whole, outs):
    width = outs[0].shape[1]
    for i, out in reversed(list(enumerate(outs))):
        cols = slice(i * width, (i + 1) * width)
        out[...] = jnp.dot(
            attended[...], whole[:, cols], preferred_element_type=F32
        ).astype(BF16)


def finish_kernel(count, terms_count, upper, starts, queries, local, weights, *refs):
    pieces, terms, refs = refs[:count], refs[count : count + terms_count], refs[count + terms_count :]
    attended, *outs = refs[:-7]
    query, sums, own_weights, own_terms, whole, sems, piece_sems = refs[-7:]
    columns = whole.shape[1]
    copies = copy_all(
        [
            pltpu.make_async_copy(array, scratch, sems.at[i])
            for i, (array, scratch) in enumerate(
                [(queries, query), (local, sums), (weights, own_weights)]
                + [(term, own_terms.at[i]) for i, term in enumerate(terms)]
            )
        ]
    )
    fetch_columns(pieces, starts, columns, whole, piece_sems, "start")
    wait_all(copies)
    heads, dim = own_terms.shape[1:3]
    first = own_weights.shape[2] - upper.shape[0]
    rows = query.shape[0]
    tile = min(256, rows)
    for low in range(0, rows, tile):
        span = slice(low, low + tile)
        for head in range(heads):
            own = slice(head * dim, (head + 1) * dim)
            total = sums[span, own]
            for i in range(terms_count):
                level = i if i < 2 else i - 1
                weight = own_weights[head, span, first + level : first + level + 1]
                total += (weight * upper[level]) * jnp.dot(
                    query[span, own], own_terms[i, head], preferred_element_type=F32
                )
            scale = lax.rsqrt(jnp.mean(total * total, axis=-1, keepdims=True) + 1e-06)
            attended[span, own] = (total * scale).astype(BF16)
    fetch_columns(pieces, starts, columns, whole, piece_sems, "wait")
    multiply_groups(attended, whole, outs)


def finish(queries, local, weights, upper, terms, starts, pieces, groups):
    rows, inner = queries.shape
    width = sum(a.size for a in pieces) // inner // groups
    count = groups // 2
    return call(
        functools.partial(finish_kernel, len(pieces), len(terms)),
        [jax.ShapeDtypeStruct(queries.shape, BF16)]
        + [jax.ShapeDtypeStruct((rows, width), BF16)] * count,
        [upper, starts, queries, local, weights, *pieces, *terms],
        [
            pltpu.VMEM(queries.shape, BF16),
            pltpu.VMEM(local.shape, F32),
            pltpu.VMEM(weights.shape, F32),
            pltpu.VMEM((len(terms), *terms[0].shape), BF16),
            pltpu.VMEM((inner, width * count), BF16),
            *semaphores(3 + len(terms), len(pieces)),
        ],
        in_specs=[SMEM] * 2 + [HBM] * (3 + len(pieces) + len(terms)),
        out_specs=[WHOLE(queries.shape)] + [WHOLE((rows, width))] * count,
        grid=(1,),
    )


def output_kernel(count, starts, attended, *refs):
    pieces, (*outs, whole, sems) = refs[:count], refs[count:]
    for act in ("start", "wait"):
        fetch_columns(pieces, starts, 0, whole, sems, act)
    multiply_groups(attended, whole, outs)


def output(attended, starts, pieces, groups):
    rows, inner = attended.shape
    width = sum(a.size for a in pieces) // inner // groups
    count = groups // 2
    return call(
        functools.partial(output_kernel, len(pieces)),
        [jax.ShapeDtypeStruct((rows, width), BF16)] * count,
        [starts, attended, *pieces],
        [pltpu.VMEM((inner, width * count), BF16), *semaphores(len(pieces))],
        in_specs=[SMEM, WHOLE((rows, inner))] + [HBM] * len(pieces),
        out_specs=[WHOLE((rows, width))] * count,
        grid=(1,),
    )


def per_device(tokens, w_query, w_key, w_value, w_out, level_weights):
    n = lax.axis_size("seq")
    groups = lax.axis_size("head")
    here = lax.axis_index("seq")
    group = lax.axis_index("head")
    local_bits = tokens.shape[0].bit_length() - 1
    heads = level_weights.shape[0]
    ringed = n <= LONGEST_RING and n % 2 == 0

    share = n // groups
    depth, width = w_query.shape[0], w_out.shape[1]
    bits = n.bit_length() - 1
    upper = jnp.stack([here >> bit & 1 for bit in range(bits)]).astype(F32)
    weights_by_token = level_weights.transpose(0, 2, 1)
    if ringed:
        owners = piece_owners(n)
        key, value, query, out = [
            Ring(w, n, i % 2) for i, w in enumerate((w_key, w_value, w_query, w_out))
        ]
        starts = table([(owner * depth, 0) for owner in owners])
        out_starts = table(
            [(0, ((g // share ^ group) * share + g % share) * width) for g in owners]
        )
        mixing = mixing_matrix(weights_by_token, local_bits)
        mixing, starts, out_starts, upper = lax.optimization_barrier(
            (mixing, starts, out_starts, upper)
        )
        for step in range(1, n // 2 + 1):
            key.advance(*((mixing,) if step == 2 else ()))
            value.advance()
            query.advance()
            if step > 1:
                out.advance(*(key.gate if step == 2 else ()))
        pieces = [ring.pieces for ring in (key, value, query)]
    else:
        mixing = mixing_matrix(weights_by_token, local_bits)
        pieces = [
            [lax.all_gather(w, "seq", axis=0, tiled=True)] for w in (w_key, w_value, w_query)
        ]
        starts = table([(0, 0)])
    *pieces, query_pieces = pieces
    keys, values, running, rounded = project_keys_values(tokens, starts, *pieces, heads)

    def from_partner(array, apart):
        return lax.ppermute(array, "seq", [(i, i ^ apart) for i in range(n)])

    terms = [from_partner(rounded, apart) for apart in (1, 2, 3)]
    for bit in range(2, bits):
        for term in terms[-3:] if bit == 2 else terms[-1:]:
            running = running + term.astype(F32)
        terms = terms + [from_partner(running.astype(BF16), 1 << bit)]
    tokens = after(tokens, [running])
    queries, local = attend_locally(tokens, starts, query_pieces, keys, values, mixing)
    if ringed:
        out.advance(rounded)
        out_pieces = out.pieces
    else:
        whole = lax.all_gather(w_out, "seq", axis=1, tiled=True)
        width *= share
        out_pieces = [
            lax.dynamic_slice_in_dim(whole, (group ^ k) * width, width, 1) for k in range(groups)
        ]
        out_starts = table([(0, k * width) for k in range(groups)])

    far = groups.bit_length() - 2

    def from_group(array, bit):
        return lax.ppermute(array, "head", [(g, g ^ 1 << bit) for g in range(groups)])

    def sum_near(shares, kind):
        for bit in range(far):
            theirs = {k ^ 1 << bit: from_group(a, bit) for k, a in shares.items() if k >> bit & 1}
            shares = {
                k: (shares[k].astype(F32) + a.astype(F32)).astype(kind) for k, a in theirs.items()
            }
        (total,) = shares.values()
        return total

    attended, *shares = finish(
        queries, local, weights_by_token, upper, terms, out_starts, out_pieces, groups
    )
    away = sum_near({groups // 2 + k: a for k, a in enumerate(shares)}, BF16)
    theirs = from_group(away, far)
    shares = output(after(attended, [away]), out_starts, out_pieces, groups)
    ours = sum_near(dict(enumerate(shares)), F32)
    return (ours.astype(F32) + theirs.astype(F32)).astype(BF16)


def solution(mesh):
    in_specs = (
        P("seq", None),
        P("seq", "head"),
        P("seq", "head"),
        P("seq", "head"),
        P("head", "seq"),
        P("head", None, "seq"),
    )
    out_specs = P("seq", "head")
    return jax.shard_map(
        per_device, mesh=mesh, in_specs=in_specs, out_specs=out_specs, check_vma=False
    )
```

```python
import functools

import jax
import jax.numpy as jnp
from jax import lax
from jax.experimental import pallas as pl
from jax.experimental.pallas import tpu as pltpu
from jax.sharding import PartitionSpec as P

F32, BF16 = jnp.float32, jnp.bfloat16
LONGEST_RING = 16
SLOWER = 4
VMEM_BYTES = 56 * 2**20
END_BYTES = 24 * 2**20
VMEM = pl.BlockSpec(memory_space=pltpu.VMEM)
HBM = pl.BlockSpec(memory_space=pl.ANY)
WHOLE = lambda shape: pl.BlockSpec(shape, lambda *_: (0,) * len(shape))
SMEM = pl.BlockSpec(memory_space=pltpu.SMEM)


def call(kernel, outs, operands, scratch=(), grant=VMEM_BYTES, **grid):
    nbytes = sum(a.size * a.dtype.itemsize for a in (*operands, *outs))
    return pl.pallas_call(
        kernel,
        out_shape=outs,
        scratch_shapes=list(scratch),
        compiler_params=pltpu.CompilerParams(vmem_limit_bytes=grant),
        cost_estimate=pl.CostEstimate(
            flops=1, bytes_accessed=SLOWER * nbytes, transcendentals=0
        ),
        **grid,
    )(*operands)


def ring_order(n):
    return list(range(0, n, 2)) + list(range(n - 1, 0, -2))


def ring_position(index, n):
    return jnp.where(index % 2 == 0, index // 2, n - 1 - index // 2)


def ring_owner(position, n):
    position = (position + n) % n
    return jnp.where(position < n // 2, 2 * position, 2 * (n - 1 - position) + 1)


class Ring:
    def __init__(self, piece, n, opposite):
        order = ring_order(n)
        self.n, self.opposite, self.step = n, opposite, 0
        self.onward = [(order[i], order[(i + 1) % n]) for i in range(n)]
        self.back = [(b, a) for a, b in self.onward]
        self.here = ring_position(lax.axis_index("seq"), n)
        self.ways = [piece, piece]
        self.pieces = [(piece, lax.axis_index("seq"))]
        self.gate = ()

    def advance(self, *gate):
        self.step += 1
        self.gate = tuple(self.ways)
        last = self.step == self.n // 2
        for way, pairs in enumerate((self.onward, self.back)):
            if last and self.opposite != way:
                continue
            piece = self.ways[way]
            self.ways[way] = lax.ppermute(after(piece, gate), "seq", pairs)
            owner = ring_owner(self.here + (self.step if way else -self.step), self.n)
            self.pieces.append((self.ways[way], owner))


def after(array, others):
    return lax.optimization_barrier((array, *others))[0] if others else array


def copy_all(copies):
    for copy in copies:
        copy.start()
    return copies


def fetch(pieces, starts, whole, sems, cols=None):
    copies = []
    for i, piece in enumerate(pieces):
        piece = piece if cols is None else piece.at[:, cols]
        rows, width = piece.shape
        down = pl.ds(pl.multiple_of(starts[0, i], rows), rows)
        along = pl.ds(pl.multiple_of(starts[1, i], width), width)
        copies.append(pltpu.make_async_copy(piece, whole.at[down, along], sems.at[i]))
    return copy_all(copies)


def table(starts):
    return jnp.stack([jnp.stack([jnp.asarray(p[i], jnp.int32) for p in starts]) for i in (0, 1)])


def wait_all(copies):
    for copy in copies:
        copy.wait()


def multiply(left, right, out):
    width = min(256, out.shape[1])
    for low in range(0, out.shape[1], width):
        cols = slice(low, low + width)
        out[:, cols] = jnp.dot(left[...], right[:, cols], preferred_element_type=F32).astype(BF16)


def semaphores(*counts):
    return [pltpu.SemaphoreType.DMA((count,)) for count in counts]


def fetch_rows(array, local, sems):
    rows = local.shape[0] // sems.shape[0]
    parts = [slice(i * rows, (i + 1) * rows) for i in range(sems.shape[0])]
    return copy_all(
        [pltpu.make_async_copy(array.at[p], local.at[p], sems.at[i]) for i, p in enumerate(parts)]
    )


def key_value_kernel(count, starts, tokens, *refs):
    key_pieces, value_pieces, refs = refs[:count], refs[count : 2 * count], refs[2 * count :]
    keys, values, states, rounded, own_tokens, whole, whole_values, token_sems, sems = refs
    copies = fetch_rows(tokens, own_tokens, token_sems)
    wait_all(copies + fetch(key_pieces, starts, whole, sems.at[0]))
    copies = fetch(value_pieces, starts, whole_values, sems.at[1])
    multiply(own_tokens, whole, keys)
    wait_all(copies)
    multiply(own_tokens, whole_values, values)
    heads, dim = states.shape[:2]
    for head in range(heads):
        own = slice(head * dim, (head + 1) * dim)
        sums = lax.dot_general(
            keys[:, own], values[:, own], (((0,), (0,)), ((), ())), preferred_element_type=F32
        )
        states[head] = sums
        rounded[head] = sums.astype(BF16)


def project_keys_values(tokens, starts, key_pieces, value_pieces, heads):
    arrays = [*key_pieces, *value_pieces]
    count = len(key_pieces)
    rows, depth = tokens.shape
    width = arrays[0].shape[1]
    dim = width // heads
    shapes = [(rows, width)] * 2 + [(heads, dim, dim)] * 2
    return call(
        functools.partial(key_value_kernel, count),
        [jax.ShapeDtypeStruct(s, t) for s, t in zip(shapes, (BF16, BF16, F32, BF16))],
        [starts, tokens, *arrays],
        [
            pltpu.VMEM((rows, depth), BF16),
            *[pltpu.VMEM((depth, width), BF16)] * 2,
            *semaphores(8),
            pltpu.SemaphoreType.DMA((2, count)),
        ],
        in_specs=[SMEM] + [HBM] * (1 + len(arrays)),
        out_specs=[WHOLE(s) for s in shapes],
        grid=(1,),
    )


def local_kernel(starts, tokens, keys, values, mixing, *refs):
    *pieces, queries, local, own_tokens, whole, key, value, mix, token_sems, mix_sems, sems, more = refs
    copies = fetch_rows(tokens, own_tokens, token_sems)
    copies += fetch(pieces, starts, whole, sems)
    wait_all(copies)
    copies = fetch_rows(mixing, mix, mix_sems)
    copies += copy_all(
        [
            pltpu.make_async_copy(keys, key, more.at[0]),
            pltpu.make_async_copy(values, value, more.at[1]),
        ]
    )
    multiply(own_tokens, whole, queries)
    wait_all(copies)
    rows = queries.shape[0]
    heads = mix.shape[0]
    dim = queries.shape[1] // heads
    tile = min(256, rows)
    for head in range(heads):
        own = slice(head * dim, (head + 1) * dim)
        for low in range(0, rows, tile):
            span, seen = slice(low, low + tile), slice(0, low + tile)
            scores = lax.dot_general(
                queries[span, own],
                key[seen, own],
                (((1,), (1,)), ((), ())),
                preferred_element_type=F32,
            )
            mixed = (scores * mix[head, span, seen].astype(F32)).astype(BF16)
            local[span, own] = jnp.dot(mixed, value[seen, own], preferred_element_type=F32)


def attend_locally(tokens, starts, pieces, keys, values, mixing):
    rows, depth = tokens.shape
    shape = keys.shape
    return call(
        local_kernel,
        [jax.ShapeDtypeStruct(shape, BF16), jax.ShapeDtypeStruct(shape, F32)],
        [starts, tokens, keys, values, mixing, *pieces],
        [
            pltpu.VMEM((rows, depth), BF16),
            pltpu.VMEM((depth, shape[1]), BF16),
            *[pltpu.VMEM(shape, BF16)] * 2,
            pltpu.VMEM(mixing.shape, BF16),
            *semaphores(8, mixing.shape[0], len(pieces), 2),
        ],
        in_specs=[SMEM] + [HBM] * (4 + len(pieces)),
        out_specs=[WHOLE(shape)] * 2,
        grid=(1,),
    )


def mixing_kernel(bits, weights, mixing):
    rows = mixing.shape[1]
    tile = min(256, rows)
    tile_bits = tile.bit_length() - 1
    column = lambda level, low: weights[0, low : low + tile, level : level + 1]
    t = lax.broadcasted_iota(jnp.int32, (tile, tile), 0)
    s = lax.broadcasted_iota(jnp.int32, (tile, tile), 1)
    apart = jnp.bitwise_xor(t, s)
    for low in range(0, rows, tile):
        for left in range(0, low, tile):
            level = tile_bits + ((low // tile) ^ (left // tile)).bit_length()
            mixing[0, low : low + tile, left : left + tile] = jnp.broadcast_to(
                column(level, low), (tile, tile)
            ).astype(BF16)
        mixed = jnp.broadcast_to(column(0, low), (tile, tile))
        for level in range(1, tile_bits + 1):
            mixed = jnp.where(apart >= 1 << (level - 1), column(level, low), mixed)
        mixing[0, low : low + tile, low : low + tile] = jnp.where(s <= t, mixed, 0.0).astype(BF16)


def mixing_matrix(weights_by_token, bits):
    heads, rows, levels = weights_by_token.shape
    return call(
        functools.partial(mixing_kernel, bits),
        [jax.ShapeDtypeStruct((heads, rows, rows), BF16)],
        [weights_by_token],
        grid=(heads,),
        in_specs=[pl.BlockSpec((1, rows, levels), lambda h: (h, 0, 0))],
        out_specs=[pl.BlockSpec((1, rows, rows), lambda h: (h, 0, 0))],
    )[0]


def fetch_columns(pieces, starts, low, whole, sems, act):
    for i, piece in enumerate(pieces):
        column = starts[1, i] - low

        @pl.when((column >= 0) & (column < whole.shape[1]))
        def _():
            along = pl.ds(pl.multiple_of(column, piece.shape[1]), piece.shape[1])
            getattr(pltpu.make_async_copy(piece, whole.at[:, along], sems.at[i]), act)()


def multiply_groups(attended, whole, outs):
    width = outs[0].shape[1]
    for i, out in reversed(list(enumerate(outs))):
        cols = slice(i * width, (i + 1) * width)
        out[...] = jnp.dot(
            attended[...], whole[:, cols], preferred_element_type=F32
        ).astype(BF16)


def finish_kernel(count, terms_count, upper, starts, queries, local, weights, *refs):
    pieces, terms, refs = refs[:count], refs[count : count + terms_count], refs[count + terms_count :]
    attended, *outs = refs[:-7]
    query, sums, own_weights, own_terms, whole, sems, piece_sems = refs[-7:]
    columns = whole.shape[1]
    copies = copy_all(
        [
            pltpu.make_async_copy(array, scratch, sems.at[i])
            for i, (array, scratch) in enumerate(
                [(queries, query), (local, sums), (weights, own_weights)]
                + [(term, own_terms.at[i]) for i, term in enumerate(terms)]
            )
        ]
    )
    fetch_columns(pieces, starts, columns, whole, piece_sems, "start")
    wait_all(copies)
    heads, dim = own_terms.shape[1:3]
    first = own_weights.shape[2] - upper.shape[0]
    rows = query.shape[0]
    tile = min(256, rows)
    for low in range(0, rows, tile):
        span = slice(low, low + tile)
        for head in range(heads):
            own = slice(head * dim, (head + 1) * dim)
            total = sums[span, own]
            for i in range(terms_count):
                level = i if i < 2 else i - 1
                weight = own_weights[head, span, first + level : first + level + 1]
                total += (weight * upper[level]) * jnp.dot(
                    query[span, own], own_terms[i, head], preferred_element_type=F32
                )
            scale = lax.rsqrt(jnp.mean(total * total, axis=-1, keepdims=True) + 1e-06)
            attended[span, own] = (total * scale).astype(BF16)
    fetch_columns(pieces, starts, columns, whole, piece_sems, "wait")
    multiply_groups(attended, whole, outs)


def finish(queries, local, weights, upper, terms, starts, pieces, groups):
    rows, inner = queries.shape
    width = sum(a.size for a in pieces) // inner // groups
    count = groups // 2
    return call(
        functools.partial(finish_kernel, len(pieces), len(terms)),
        [jax.ShapeDtypeStruct(queries.shape, BF16)]
        + [jax.ShapeDtypeStruct((rows, width), BF16)] * count,
        [upper, starts, queries, local, weights, *pieces, *terms],
        [
            pltpu.VMEM(queries.shape, BF16),
            pltpu.VMEM(local.shape, F32),
            pltpu.VMEM(weights.shape, F32),
            pltpu.VMEM((len(terms), *terms[0].shape), BF16),
            pltpu.VMEM((inner, width * count), BF16),
            *semaphores(3 + len(terms), len(pieces)),
        ],
        in_specs=[SMEM] * 2 + [HBM] * (3 + len(pieces) + len(terms)),
        out_specs=[WHOLE(queries.shape)] + [WHOLE((rows, width))] * count,
        grant=END_BYTES,
        grid=(1,),
    )


def output_kernel(count, starts, attended, *refs):
    pieces, (*outs, whole, sems) = refs[:count], refs[count:]
    for act in ("start", "wait"):
        fetch_columns(pieces, starts, 0, whole, sems, act)
    multiply_groups(attended, whole, outs)


def output(attended, starts, pieces, groups):
    rows, inner = attended.shape
    width = sum(a.size for a in pieces) // inner // groups
    count = groups // 2
    return call(
        functools.partial(output_kernel, len(pieces)),
        [jax.ShapeDtypeStruct((rows, width), BF16)] * count,
        [starts, attended, *pieces],
        [pltpu.VMEM((inner, width * count), BF16), *semaphores(len(pieces))],
        in_specs=[SMEM, WHOLE((rows, inner))] + [HBM] * len(pieces),
        out_specs=[WHOLE((rows, width))] * count,
        grant=END_BYTES,
        grid=(1,),
    )


def per_device(tokens, w_query, w_key, w_value, w_out, level_weights):
    n = lax.axis_size("seq")
    groups = lax.axis_size("head")
    here = lax.axis_index("seq")
    group = lax.axis_index("head")
    local_bits = tokens.shape[0].bit_length() - 1
    heads = level_weights.shape[0]
    ringed = n <= LONGEST_RING and n % 2 == 0

    share = n // groups
    depth, width = w_query.shape[0], w_out.shape[1]
    bits = n.bit_length() - 1
    upper = jnp.stack([here >> bit & 1 for bit in range(bits)]).astype(F32)
    weights_by_token = level_weights.transpose(0, 2, 1)
    if ringed:
        key, value, query, out = [
            Ring(w, n, i % 2) for i, w in enumerate((w_key, w_value, w_query, w_out))
        ]
        mixing = mixing_matrix(weights_by_token, local_bits)
        for step in range(1, n // 2 + 1):
            key.advance(*((mixing,) if step == 3 else ()))
            value.advance()
            query.advance()
            if step > 1:
                out.advance(*(key.gate if step == 2 else ()))
        pieces = [[a for a, _ in ring.pieces] for ring in (key, value, query)]
        starts = table([(owner * depth, 0) for _, owner in key.pieces])
    else:
        mixing = mixing_matrix(weights_by_token, local_bits)
        pieces = [
            [lax.all_gather(w, "seq", axis=0, tiled=True)] for w in (w_key, w_value, w_query)
        ]
        starts = table([(0, 0)])
    *pieces, query_pieces = pieces
    keys, values, running, rounded = project_keys_values(tokens, starts, *pieces, heads)

    def from_partner(array, apart):
        return lax.ppermute(array, "seq", [(i, i ^ apart) for i in range(n)])

    terms = [from_partner(rounded, apart) for apart in (1, 2, 3)]
    for bit in range(2, bits):
        for term in terms[-3:] if bit == 2 else terms[-1:]:
            running = running + term.astype(F32)
        terms = terms + [from_partner(running.astype(BF16), 1 << bit)]
    tokens = after(tokens, [running])
    queries, local = attend_locally(tokens, starts, query_pieces, keys, values, mixing)
    if ringed:
        out.advance(rounded)
        out_pieces = [a for a, _ in out.pieces]
        out_starts = [
            (0, ((owner // share ^ group) * share + owner % share) * width)
            for _, owner in out.pieces
        ]
    else:
        whole = lax.all_gather(w_out, "seq", axis=1, tiled=True)
        width *= share
        out_pieces = [
            lax.dynamic_slice_in_dim(whole, (group ^ k) * width, width, 1) for k in range(groups)
        ]
        out_starts = [(0, k * width) for k in range(groups)]

    far = groups.bit_length() - 2

    def from_group(array, bit):
        return lax.ppermute(array, "head", [(g, g ^ 1 << bit) for g in range(groups)])

    def sum_near(shares, kind):
        for bit in range(far):
            theirs = {k ^ 1 << bit: from_group(a, bit) for k, a in shares.items() if k >> bit & 1}
            shares = {
                k: (shares[k].astype(F32) + a.astype(F32)).astype(kind) for k, a in theirs.items()
            }
        (total,) = shares.values()
        return total

    starts = table(out_starts)
    attended, *shares = finish(
        queries, local, weights_by_token, upper, terms, starts, out_pieces, groups
    )
    away = sum_near({groups // 2 + k: a for k, a in enumerate(shares)}, BF16)
    theirs = from_group(away, far)
    shares = output(after(attended, [away]), starts, out_pieces, groups)
    ours = sum_near(dict(enumerate(shares)), F32)
    return (ours.astype(F32) + theirs.astype(F32)).astype(BF16)


def solution(mesh):
    in_specs = (
        P("seq", None),
        P("seq", "head"),
        P("seq", "head"),
        P("seq", "head"),
        P("head", "seq"),
        P("head", None, "seq"),
    )
    out_specs = P("seq", "head")
    return jax.shard_map(
        per_device, mesh=mesh, in_specs=in_specs, out_specs=out_specs, check_vma=False
    )
```

```python
import functools

import jax
import jax.numpy as jnp
from jax import lax
from jax.experimental import pallas as pl
from jax.experimental.pallas import tpu as pltpu
from jax.sharding import PartitionSpec as P

F32, BF16 = jnp.float32, jnp.bfloat16
LONGEST_RING = 16
SLOWER = 4
VMEM_BYTES = 56 * 2**20
END_BYTES = 24 * 2**20
VMEM = pl.BlockSpec(memory_space=pltpu.VMEM)
HBM = pl.BlockSpec(memory_space=pl.ANY)
WHOLE = lambda shape: pl.BlockSpec(shape, lambda *_: (0,) * len(shape))
SMEM = pl.BlockSpec(memory_space=pltpu.SMEM)


def call(kernel, outs, operands, scratch=(), grant=VMEM_BYTES, **grid):
    nbytes = sum(a.size * a.dtype.itemsize for a in (*operands, *outs))
    return pl.pallas_call(
        kernel,
        out_shape=outs,
        scratch_shapes=list(scratch),
        compiler_params=pltpu.CompilerParams(vmem_limit_bytes=grant),
        cost_estimate=pl.CostEstimate(
            flops=1, bytes_accessed=SLOWER * nbytes, transcendentals=0
        ),
        **grid,
    )(*operands)


def ring_order(n):
    return list(range(0, n, 2)) + list(range(n - 1, 0, -2))


def ring_position(index, n):
    return jnp.where(index % 2 == 0, index // 2, n - 1 - index // 2)


def ring_owner(position, n):
    position = (position + n) % n
    return jnp.where(position < n // 2, 2 * position, 2 * (n - 1 - position) + 1)


class Ring:
    def __init__(self, piece, n, opposite):
        order = ring_order(n)
        self.n, self.opposite, self.step = n, opposite, 0
        self.onward = [(order[i], order[(i + 1) % n]) for i in range(n)]
        self.back = [(b, a) for a, b in self.onward]
        self.here = ring_position(lax.axis_index("seq"), n)
        self.ways = [piece, piece]
        self.pieces = [(piece, lax.axis_index("seq"))]
        self.gate = ()

    def advance(self, *gate):
        self.step += 1
        self.gate = tuple(self.ways)
        last = self.step == self.n // 2
        for way, pairs in enumerate((self.onward, self.back)):
            if last and self.opposite != way:
                continue
            piece = self.ways[way]
            self.ways[way] = lax.ppermute(after(piece, gate), "seq", pairs)
            owner = ring_owner(self.here + (self.step if way else -self.step), self.n)
            self.pieces.append((self.ways[way], owner))


def after(array, others):
    return lax.optimization_barrier((array, *others))[0] if others else array


def copy_all(copies):
    for copy in copies:
        copy.start()
    return copies


def fetch(pieces, starts, whole, sems, cols=None):
    copies = []
    for i, piece in enumerate(pieces):
        piece = piece if cols is None else piece.at[:, cols]
        rows, width = piece.shape
        down = pl.ds(pl.multiple_of(starts[0, i], rows), rows)
        along = pl.ds(pl.multiple_of(starts[1, i], width), width)
        copies.append(pltpu.make_async_copy(piece, whole.at[down, along], sems.at[i]))
    return copy_all(copies)


def table(starts):
    return jnp.stack([jnp.stack([jnp.asarray(p[i], jnp.int32) for p in starts]) for i in (0, 1)])


def wait_all(copies):
    for copy in copies:
        copy.wait()


def multiply(left, right, out):
    width = min(256, out.shape[1])
    for low in range(0, out.shape[1], width):
        cols = slice(low, low + width)
        out[:, cols] = jnp.dot(left[...], right[:, cols], preferred_element_type=F32).astype(BF16)


def semaphores(*counts):
    return [pltpu.SemaphoreType.DMA((count,)) for count in counts]


def fetch_rows(array, local, sems):
    rows = local.shape[0] // sems.shape[0]
    parts = [slice(i * rows, (i + 1) * rows) for i in range(sems.shape[0])]
    return copy_all(
        [pltpu.make_async_copy(array.at[p], local.at[p], sems.at[i]) for i, p in enumerate(parts)]
    )


def key_value_kernel(count, starts, tokens, *refs):
    key_pieces, value_pieces, refs = refs[:count], refs[count : 2 * count], refs[2 * count :]
    keys, values, states, rounded, own_tokens, whole, whole_values, token_sems, sems = refs
    copies = fetch_rows(tokens, own_tokens, token_sems)
    wait_all(copies + fetch(key_pieces, starts, whole, sems.at[0]))
    copies = fetch(value_pieces, starts, whole_values, sems.at[1])
    multiply(own_tokens, whole, keys)
    wait_all(copies)
    multiply(own_tokens, whole_values, values)
    heads, dim = states.shape[:2]
    for head in range(heads):
        own = slice(head * dim, (head + 1) * dim)
        sums = lax.dot_general(
            keys[:, own], values[:, own], (((0,), (0,)), ((), ())), preferred_element_type=F32
        )
        states[head] = sums
        rounded[head] = sums.astype(BF16)


def project_keys_values(tokens, starts, key_pieces, value_pieces, heads):
    arrays = [*key_pieces, *value_pieces]
    count = len(key_pieces)
    rows, depth = tokens.shape
    width = arrays[0].shape[1]
    dim = width // heads
    shapes = [(rows, width)] * 2 + [(heads, dim, dim)] * 2
    return call(
        functools.partial(key_value_kernel, count),
        [jax.ShapeDtypeStruct(s, t) for s, t in zip(shapes, (BF16, BF16, F32, BF16))],
        [starts, tokens, *arrays],
        [
            pltpu.VMEM((rows, depth), BF16),
            *[pltpu.VMEM((depth, width), BF16)] * 2,
            *semaphores(8),
            pltpu.SemaphoreType.DMA((2, count)),
        ],
        in_specs=[SMEM] + [HBM] * (1 + len(arrays)),
        out_specs=[WHOLE(s) for s in shapes],
        grid=(1,),
    )


def local_kernel(starts, tokens, keys, values, mixing, *refs):
    *pieces, queries, local, own_tokens, whole, key, value, mix, token_sems, mix_sems, sems, more = refs
    copies = fetch_rows(tokens, own_tokens, token_sems)
    copies += fetch(pieces, starts, whole, sems)
    wait_all(copies)
    copies = fetch_rows(mixing, mix, mix_sems)
    copies += copy_all(
        [
            pltpu.make_async_copy(keys, key, more.at[0]),
            pltpu.make_async_copy(values, value, more.at[1]),
        ]
    )
    multiply(own_tokens, whole, queries)
    wait_all(copies)
    rows = queries.shape[0]
    heads = mix.shape[0]
    dim = queries.shape[1] // heads
    tile = min(256, rows)
    for head in range(heads):
        own = slice(head * dim, (head + 1) * dim)
        for low in range(0, rows, tile):
            span, seen = slice(low, low + tile), slice(0, low + tile)
            scores = lax.dot_general(
                queries[span, own],
                key[seen, own],
                (((1,), (1,)), ((), ())),
                preferred_element_type=F32,
            )
            mixed = (scores * mix[head, span, seen].astype(F32)).astype(BF16)
            local[span, own] = jnp.dot(mixed, value[seen, own], preferred_element_type=F32)


def attend_locally(tokens, starts, pieces, keys, values, mixing):
    rows, depth = tokens.shape
    shape = keys.shape
    return call(
        local_kernel,
        [jax.ShapeDtypeStruct(shape, BF16), jax.ShapeDtypeStruct(shape, F32)],
        [starts, tokens, keys, values, mixing, *pieces],
        [
            pltpu.VMEM((rows, depth), BF16),
            pltpu.VMEM((depth, shape[1]), BF16),
            *[pltpu.VMEM(shape, BF16)] * 2,
            pltpu.VMEM(mixing.shape, BF16),
            *semaphores(8, mixing.shape[0], len(pieces), 2),
        ],
        in_specs=[SMEM] + [HBM] * (4 + len(pieces)),
        out_specs=[WHOLE(shape)] * 2,
        grid=(1,),
    )


def mixing_kernel(bits, weights, mixing):
    rows = mixing.shape[1]
    tile = min(256, rows)
    tile_bits = tile.bit_length() - 1
    column = lambda level, low: weights[0, low : low + tile, level : level + 1]
    t = lax.broadcasted_iota(jnp.int32, (tile, tile), 0)
    s = lax.broadcasted_iota(jnp.int32, (tile, tile), 1)
    apart = jnp.bitwise_xor(t, s)
    for low in range(0, rows, tile):
        for left in range(0, low, tile):
            level = tile_bits + ((low // tile) ^ (left // tile)).bit_length()
            mixing[0, low : low + tile, left : left + tile] = jnp.broadcast_to(
                column(level, low), (tile, tile)
            ).astype(BF16)
        mixed = jnp.broadcast_to(column(0, low), (tile, tile))
        for level in range(1, tile_bits + 1):
            mixed = jnp.where(apart >= 1 << (level - 1), column(level, low), mixed)
        mixing[0, low : low + tile, low : low + tile] = jnp.where(s <= t, mixed, 0.0).astype(BF16)


def mixing_matrix(weights_by_token, bits):
    heads, rows, levels = weights_by_token.shape
    return call(
        functools.partial(mixing_kernel, bits),
        [jax.ShapeDtypeStruct((heads, rows, rows), BF16)],
        [weights_by_token],
        grid=(heads,),
        in_specs=[pl.BlockSpec((1, rows, levels), lambda h: (h, 0, 0))],
        out_specs=[pl.BlockSpec((1, rows, rows), lambda h: (h, 0, 0))],
    )[0]


def fetch_columns(pieces, starts, low, whole, sems, act):
    for i, piece in enumerate(pieces):
        column = starts[1, i] - low

        @pl.when((column >= 0) & (column < whole.shape[1]))
        def _():
            along = pl.ds(pl.multiple_of(column, piece.shape[1]), piece.shape[1])
            getattr(pltpu.make_async_copy(piece, whole.at[:, along], sems.at[i]), act)()


def multiply_groups(attended, whole, outs):
    width = outs[0].shape[1]
    for i, out in reversed(list(enumerate(outs))):
        cols = slice(i * width, (i + 1) * width)
        out[...] = jnp.dot(
            attended[...], whole[:, cols], preferred_element_type=F32
        ).astype(BF16)


def finish_kernel(count, terms_count, upper, starts, queries, local, weights, *refs):
    pieces, terms, refs = refs[:count], refs[count : count + terms_count], refs[count + terms_count :]
    attended, *outs = refs[:-7]
    query, sums, own_weights, own_terms, whole, sems, piece_sems = refs[-7:]
    columns = whole.shape[1]
    copies = copy_all(
        [
            pltpu.make_async_copy(array, scratch, sems.at[i])
            for i, (array, scratch) in enumerate(
                [(queries, query), (local, sums), (weights, own_weights)]
                + [(term, own_terms.at[i]) for i, term in enumerate(terms)]
            )
        ]
    )
    fetch_columns(pieces, starts, columns, whole, piece_sems, "start")
    wait_all(copies)
    heads, dim = own_terms.shape[1:3]
    first = own_weights.shape[2] - upper.shape[0]
    rows = query.shape[0]
    tile = min(256, rows)
    for low in range(0, rows, tile):
        span = slice(low, low + tile)
        for head in range(heads):
            own = slice(head * dim, (head + 1) * dim)
            total = sums[span, own]
            for i in range(terms_count):
                level = i if i < 2 else i - 1
                weight = own_weights[head, span, first + level : first + level + 1]
                total += (weight * upper[level]) * jnp.dot(
                    query[span, own], own_terms[i, head], preferred_element_type=F32
                )
            scale = lax.rsqrt(jnp.mean(total * total, axis=-1, keepdims=True) + 1e-06)
            attended[span, own] = (total * scale).astype(BF16)
    fetch_columns(pieces, starts, columns, whole, piece_sems, "wait")
    multiply_groups(attended, whole, outs)


def finish(queries, local, weights, upper, terms, starts, pieces, groups):
    rows, inner = queries.shape
    width = sum(a.size for a in pieces) // inner // groups
    count = groups // 2
    return call(
        functools.partial(finish_kernel, len(pieces), len(terms)),
        [jax.ShapeDtypeStruct(queries.shape, BF16)]
        + [jax.ShapeDtypeStruct((rows, width), BF16)] * count,
        [upper, starts, queries, local, weights, *pieces, *terms],
        [
            pltpu.VMEM(queries.shape, BF16),
            pltpu.VMEM(local.shape, F32),
            pltpu.VMEM(weights.shape, F32),
            pltpu.VMEM((len(terms), *terms[0].shape), BF16),
            pltpu.VMEM((inner, width * count), BF16),
            *semaphores(3 + len(terms), len(pieces)),
        ],
        in_specs=[SMEM] * 2 + [HBM] * (3 + len(pieces) + len(terms)),
        out_specs=[WHOLE(queries.shape)] + [WHOLE((rows, width))] * count,
        grant=END_BYTES,
        grid=(1,),
    )


def output_kernel(count, starts, attended, *refs):
    pieces, (*outs, whole, sems) = refs[:count], refs[count:]
    for act in ("start", "wait"):
        fetch_columns(pieces, starts, 0, whole, sems, act)
    multiply_groups(attended, whole, outs)


def output(attended, starts, pieces, groups):
    rows, inner = attended.shape
    width = sum(a.size for a in pieces) // inner // groups
    count = groups // 2
    return call(
        functools.partial(output_kernel, len(pieces)),
        [jax.ShapeDtypeStruct((rows, width), BF16)] * count,
        [starts, attended, *pieces],
        [pltpu.VMEM((inner, width * count), BF16), *semaphores(len(pieces))],
        in_specs=[SMEM, WHOLE((rows, inner))] + [HBM] * len(pieces),
        out_specs=[WHOLE((rows, width))] * count,
        grant=END_BYTES,
        grid=(1,),
    )


def per_device(tokens, w_query, w_key, w_value, w_out, level_weights):
    n = lax.axis_size("seq")
    groups = lax.axis_size("head")
    here = lax.axis_index("seq")
    group = lax.axis_index("head")
    local_bits = tokens.shape[0].bit_length() - 1
    heads = level_weights.shape[0]
    ringed = n <= LONGEST_RING and n % 2 == 0

    share = n // groups
    depth, width = w_query.shape[0], w_out.shape[1]
    bits = n.bit_length() - 1
    upper = jnp.stack([here >> bit & 1 for bit in range(bits)]).astype(F32)
    weights_by_token = level_weights.transpose(0, 2, 1)
    if ringed:
        key, value, query, out = [
            Ring(w, n, i % 2) for i, w in enumerate((w_key, w_value, w_query, w_out))
        ]
        mixing = mixing_matrix(weights_by_token, local_bits)
        for step in range(1, n // 2 + 1):
            key.advance(*((mixing,) if step == 2 else ()))
            value.advance()
            query.advance()
            if step > 1:
                out.advance(*(key.gate if step == 2 else ()))
        pieces = [[a for a, _ in ring.pieces] for ring in (key, value, query)]
        starts = table([(owner * depth, 0) for _, owner in key.pieces])
    else:
        mixing = mixing_matrix(weights_by_token, local_bits)
        pieces = [
            [lax.all_gather(w, "seq", axis=0, tiled=True)] for w in (w_key, w_value, w_query)
        ]
        starts = table([(0, 0)])
    *pieces, query_pieces = pieces
    keys, values, running, rounded = project_keys_values(tokens, starts, *pieces, heads)

    def from_partner(array, apart):
        return lax.ppermute(array, "seq", [(i, i ^ apart) for i in range(n)])

    terms = [from_partner(rounded, apart) for apart in (1, 2, 3)]
    for bit in range(2, bits):
        for term in terms[-3:] if bit == 2 else terms[-1:]:
            running = running + term.astype(F32)
        terms = terms + [from_partner(running.astype(BF16), 1 << bit)]
    tokens = after(tokens, [running])
    queries, local = attend_locally(tokens, starts, query_pieces, keys, values, mixing)
    if ringed:
        out.advance(rounded)
        out_pieces = [a for a, _ in out.pieces]
        out_starts = [
            (0, ((owner // share ^ group) * share + owner % share) * width)
            for _, owner in out.pieces
        ]
    else:
        whole = lax.all_gather(w_out, "seq", axis=1, tiled=True)
        width *= share
        out_pieces = [
            lax.dynamic_slice_in_dim(whole, (group ^ k) * width, width, 1) for k in range(groups)
        ]
        out_starts = [(0, k * width) for k in range(groups)]

    far = groups.bit_length() - 2

    def from_group(array, bit):
        return lax.ppermute(array, "head", [(g, g ^ 1 << bit) for g in range(groups)])

    def sum_near(shares, kind):
        for bit in range(far):
            theirs = {k ^ 1 << bit: from_group(a, bit) for k, a in shares.items() if k >> bit & 1}
            shares = {
                k: (shares[k].astype(F32) + a.astype(F32)).astype(kind) for k, a in theirs.items()
            }
        (total,) = shares.values()
        return total

    starts = table(out_starts)
    attended, *shares = finish(
        queries, local, weights_by_token, upper, terms, starts, out_pieces, groups
    )
    away = sum_near({groups // 2 + k: a for k, a in enumerate(shares)}, BF16)
    theirs = from_group(away, far)
    shares = output(after(attended, [away]), starts, out_pieces, groups)
    ours = sum_near(dict(enumerate(shares)), F32)
    return (ours.astype(F32) + theirs.astype(F32)).astype(BF16)


def solution(mesh):
    in_specs = (
        P("seq", None),
        P("seq", "head"),
        P("seq", "head"),
        P("seq", "head"),
        P("head", "seq"),
        P("head", None, "seq"),
    )
    out_specs = P("seq", "head")
    return jax.shard_map(
        per_device, mesh=mesh, in_specs=in_specs, out_specs=out_specs, check_vma=False
    )
```
